32 devices in a mesh: ctx: 8 (over z, y), head: 4 (over x, core).
Axes of the slice: x: 2, y: 2, z: 4, core: 2. Of those that a mesh axis runs over, the one named last changes fastest.
Arguments:
- queries: bfloat16 [4096, 4096], P('ctx', 'head'), may hold values from -160 to 160
- key_states: bfloat16 [4096, 4096], P('ctx', 'head'), may hold values from -160 to 160
- values: bfloat16 [4096, 4096], P('ctx', 'head'), may hold values from -6 to 6
- query_gain: bfloat16 [4096], P('head'), may hold values from 0.25 to 1.75
- key_gain: bfloat16 [4096], P('head'), may hold values from 0.25 to 1.75
- memory_blocks: int32 [8, 8], replicated, may hold values from 0 to 31, as said below
- cotangent: bfloat16 [4096, 4096], P('ctx', 'head'), may hold values from -6 to 6
Outputs:
- attended: bfloat16 [4096, 4096], P('ctx', 'head')
- query_grads: bfloat16 [4096, 4096], P('ctx', 'head')
- key_grads: bfloat16 [4096, 4096], P('ctx', 'head')
- value_grads: bfloat16 [4096, 4096], P('ctx', 'head')
The draws below stay inside these ranges and needn't reach their ends.
Inputs may be any that keep to these rules, and one draw needn't show every extreme that they name: `memory_blocks`: row c lists the 8 blocks read by the tokens of ctx index c; block b holds tokens 128 b to 128 b + 127, and the 8 blocks of one row lie on 8 different ctx indices.
All inputs are finite; a program needn't handle non-finite values.
Results may differ from the reference program's by a relative error of at most 0.0045.
The reference program's roundings to bfloat16 on the way count: a program that leaves them out, or rounds other values in their place, can miss the bound.
Values may be sent and summed in bfloat16 or wider, within the bound.
A program may use at most 128 MiB of HBM per device.

```python
import math
from functools import partial
import jax
import jax.numpy as jnp
from jax import lax

HEADS = 32
DH = 128
D = 4096
SEG = 512
LEVELS = 4
BLOCK = 128
NB = 8
TOKENS = 4096


def feature_scales(base_key, slope_value):
    position = (jnp.arange(HEADS * DH) // DH).astype(jnp.float32) / max(HEADS - 1, 1)
    jitter = jax.random.uniform(base_key, (HEADS * DH,), jnp.float32, -0.5, 0.5)
    return jnp.exp(slope_value * position + jitter)


def token_scales(base_key):
    return jnp.exp(jax.random.uniform(base_key, (TOKENS,), jnp.float32, math.log(0.3), math.log(3.0)))


def draw_pair(key):
    key_list = jax.random.split(jax.random.fold_in(key, 4242), 8)
    width_all = HEADS * DH
    slope_value = math.log(3.0)
    raw_query = jnp.clip(jax.random.normal(key_list[2], (TOKENS, width_all), jnp.float32), -4.0, 4.0)
    raw_key = jnp.clip(jax.random.normal(key_list[3], (TOKENS, width_all), jnp.float32), -4.0, 4.0)
    query_array = raw_query * token_scales(key_list[4])[:, None] * feature_scales(key_list[5], slope_value)[None, :]
    key_array = raw_key * token_scales(key_list[6])[:, None] * feature_scales(key_list[7], slope_value)[None, :]
    return (query_array, key_array)


def draw_queries(key, part):
    return draw_pair(key)[0].astype(jnp.bfloat16)


def draw_key_states(key, part):
    return draw_pair(key)[1].astype(jnp.bfloat16)


def put_first(row_values, target):
    position = jnp.argmax(row_values == target)
    return row_values.at[position].set(row_values[0]).at[0].set(target)


def draw_memory_blocks(key, part):
    reader_count = TOKENS // SEG
    block_count = SEG // BLOCK
    first_key, second_key = jax.random.split(jax.random.fold_in(key, 77))
    row_keys = jax.random.split(first_key, reader_count)

    def one_row(row_key):
        return jax.random.permutation(row_key, reader_count).astype(jnp.int32)
    owners = jax.vmap(one_row)(row_keys)
    owners = owners.at[0].set(put_first(owners[0], reader_count - 1))
    owners = owners.at[1].set(put_first(owners[1], 0))
    local_ids = jax.random.randint(second_key, (reader_count, NB), 0, block_count).astype(jnp.int32)
    local_ids = local_ids.at[0, 0].set(block_count - 1).at[1, 0].set(0)
    return (owners[:, :NB] * block_count + local_ids).astype(jnp.int32)


def levels(own_key, dims, cuts, smallest, top_value):
    factor_of = 1.0
    for dim, shards_of in cuts:
        heights = jax.random.uniform(jax.random.fold_in(jax.random.fold_in(own_key, 6), dim), (shards_of,), jnp.float32, smallest / len(cuts), top_value / len(cuts))
        factor_of = factor_of * jnp.repeat(jnp.exp(heights), dims[dim] // shards_of).reshape((-1,) + (1,) * (len(dims) - 1 - dim))
    return factor_of


def normal_values(key, shape, spread, limit, cuts=(), kind=jnp.bfloat16):
    drawn = spread * jax.random.normal(key, shape, jnp.float32)
    if cuts:
        drawn = drawn * levels(key, shape, cuts, -0.22, 0.18)
    return jnp.clip(drawn, -limit, limit).astype(kind)


def setup_inputs(seed: int = 0) -> dict:
    splits = jax.random.split(jax.random.key(seed), 8)
    queries = draw_queries(jax.random.fold_in(splits[7], 71), 0)
    key_states = draw_key_states(jax.random.fold_in(splits[7], 71), 0)
    values = normal_values(splits[2], (TOKENS, D), 1.0, 6.0, ((0, 8), (1, 4)))
    query_gain = jnp.clip(1.0 + 0.15 * jax.random.normal(splits[3], (D,), jnp.float32), 0.25, 1.75).astype(jnp.bfloat16)
    key_gain = jnp.clip(1.0 + 0.15 * jax.random.normal(splits[4], (D,), jnp.float32), 0.25, 1.75).astype(jnp.bfloat16)
    memory_blocks = draw_memory_blocks(jax.random.fold_in(splits[7], 71), 0)
    cotangent = normal_values(splits[6], (TOKENS, D), 1.0, 6.0, ((0, 8), (1, 4)))
    return {"queries": queries, "key_states": key_states, "values": values, "query_gain": query_gain, "key_gain": key_gain, "memory_blocks": memory_blocks, "cotangent": cotangent}


EPSILON = 1e-06
FLOOR_SCORE = -1e+30

def round_trip(array):
    return lax.optimization_barrier(array.astype(jnp.bfloat16)).astype(jnp.float32)

def take_level(array, seg_count, stride, offset):
    shaped = array.reshape((seg_count, SEG, stride) + array.shape[1:])
    return lax.dynamic_index_in_dim(shaped, offset, 2, keepdims=False)

def put_level(block_values, seg_count, stride, offset, fill):
    filled = jnp.full((seg_count, SEG, stride) + block_values.shape[2:], fill, block_values.dtype)
    filled = lax.dynamic_update_slice_in_dim(filled, block_values[:, :, None], offset, 2)
    return filled.reshape((TOKENS,) + block_values.shape[2:])

def forward_block(query_rows, key_rows, value_rows, score_scale):
    scores = jnp.einsum('nqd,nkd->nqk', query_rows.astype(jnp.float32), key_rows.astype(jnp.float32)) * score_scale
    row_max = lax.optimization_barrier(jnp.max(scores, axis=2))
    weights = jnp.exp(scores - row_max[:, :, None])
    row_total = lax.optimization_barrier(jnp.sum(weights, axis=2))
    summed = jnp.einsum('nqk,nkd->nqd', round_trip(weights), value_rows.astype(jnp.float32))
    return (row_max, row_total, summed)

def backward_block(query_rows, key_rows, value_rows, grad_rows, log_sum, delta_rows, score_scale):
    scores = jnp.einsum('nqd,nkd->nqk', query_rows.astype(jnp.float32), key_rows.astype(jnp.float32)) * score_scale
    softmax_rows = jnp.exp(scores - log_sum[:, :, None])
    grad_softmax = jnp.einsum('nqd,nkd->nqk', grad_rows.astype(jnp.float32), value_rows.astype(jnp.float32))
    grad_scores = round_trip(softmax_rows * (grad_softmax - delta_rows[:, :, None]))
    grad_query = jnp.einsum('nqk,nkd->nqd', grad_scores, key_rows.astype(jnp.float32)) * score_scale
    grad_key = jnp.einsum('nqk,nqd->nkd', grad_scores, query_rows.astype(jnp.float32)) * score_scale
    grad_value = jnp.einsum('nqk,nqd->nkd', round_trip(softmax_rows), grad_rows.astype(jnp.float32))
    return (grad_query, grad_key, grad_value)

def head_pass(head_index, query_head, key_head, value_head, grad_head, memory_blocks, score_scale):
    reader_count = TOKENS // SEG
    block_total = TOKENS // BLOCK
    layouts = []
    for level_index in range(LEVELS):
        stride = 2 ** level_index
        layouts.append((TOKENS // (SEG * stride), stride, head_index % stride))
    part_max = []
    part_total = []
    part_sum = []
    for seg_count, stride, offset in layouts:
        take_rows = partial(take_level, seg_count=seg_count, stride=stride, offset=offset)
        row_max, row_total, summed = forward_block(take_rows(query_head), take_rows(key_head), take_rows(value_head), score_scale)
        part_max.append(put_level(row_max, seg_count, stride, offset, FLOOR_SCORE))
        part_total.append(put_level(row_total, seg_count, stride, offset, 0.0))
        part_sum.append(put_level(summed, seg_count, stride, offset, 0.0))
    memory_keys = key_head.reshape(block_total, BLOCK, DH)[memory_blocks].reshape(reader_count, NB * BLOCK, DH)
    memory_values = value_head.reshape(block_total, BLOCK, DH)[memory_blocks].reshape(reader_count, NB * BLOCK, DH)
    memory_queries = query_head.reshape(reader_count, SEG, DH)
    row_max, row_total, summed = forward_block(memory_queries, memory_keys, memory_values, score_scale)
    part_max.append(row_max.reshape(TOKENS))
    part_total.append(row_total.reshape(TOKENS))
    part_sum.append(summed.reshape(TOKENS, DH))
    joint_max = lax.optimization_barrier(jnp.max(jnp.stack(part_max), axis=0))
    joint_total = jnp.zeros((TOKENS,), jnp.float32)
    numerator = jnp.zeros((TOKENS, DH), jnp.float32)
    for part_index in range(len(part_max)):
        factor = jnp.exp(part_max[part_index] - joint_max)
        joint_total = joint_total + factor * part_total[part_index]
        numerator = numerator + factor[:, None] * part_sum[part_index]
    merged = numerator / joint_total[:, None]
    log_sum = joint_max + jnp.log(joint_total)
    delta_full = lax.optimization_barrier(jnp.sum(grad_head.astype(jnp.float32) * merged, axis=1))
    grad_query_total = jnp.zeros((TOKENS, DH), jnp.float32)
    grad_key_total = jnp.zeros((TOKENS, DH), jnp.float32)
    grad_value_total = jnp.zeros((TOKENS, DH), jnp.float32)
    for seg_count, stride, offset in layouts:
        take_rows = partial(take_level, seg_count=seg_count, stride=stride, offset=offset)
        grad_query, grad_key, grad_value = backward_block(take_rows(query_head), take_rows(key_head), take_rows(value_head), take_rows(grad_head), take_rows(log_sum), take_rows(delta_full), score_scale)
        grad_query_total = grad_query_total + put_level(grad_query, seg_count, stride, offset, 0.0)
        grad_key_total = grad_key_total + put_level(grad_key, seg_count, stride, offset, 0.0)
        grad_value_total = grad_value_total + put_level(grad_value, seg_count, stride, offset, 0.0)
    grad_query, grad_key, grad_value = backward_block(memory_queries, memory_keys, memory_values, grad_head.reshape(reader_count, SEG, DH), log_sum.reshape(reader_count, SEG), delta_full.reshape(reader_count, SEG), score_scale)
    grad_query_total = grad_query_total + grad_query.reshape(TOKENS, DH)
    key_back = jnp.zeros((block_total, BLOCK, DH), jnp.float32).at[memory_blocks].add(round_trip(grad_key).reshape(reader_count, NB, BLOCK, DH))
    value_back = jnp.zeros((block_total, BLOCK, DH), jnp.float32).at[memory_blocks].add(round_trip(grad_value).reshape(reader_count, NB, BLOCK, DH))
    grad_key_total = grad_key_total + key_back.reshape(TOKENS, DH)
    grad_value_total = grad_value_total + value_back.reshape(TOKENS, DH)
    return (merged, grad_query_total, grad_key_total, grad_value_total)

def reference(queries, key_states, values, query_gain, key_gain, memory_blocks, cotangent):
    score_scale = 1.0 / math.sqrt(DH)
    query_float = queries.astype(jnp.float32)
    key_float = key_states.astype(jnp.float32)
    query_inverse = lax.rsqrt(lax.optimization_barrier(jnp.mean(query_float * query_float, axis=1, keepdims=True)) + EPSILON)
    key_inverse = lax.rsqrt(lax.optimization_barrier(jnp.mean(key_float * key_float, axis=1, keepdims=True)) + EPSILON)
    query_normed = (query_float * query_inverse * query_gain.astype(jnp.float32)).astype(jnp.bfloat16)
    key_normed = (key_float * key_inverse * key_gain.astype(jnp.float32)).astype(jnp.bfloat16)

    def split_heads(array):
        return array.reshape(TOKENS, HEADS, DH).transpose(1, 0, 2)

    def join_heads(array):
        return array.transpose(1, 0, 2).reshape(TOKENS, HEADS * DH)

    def one_head(head_item):
        head_index, query_head, key_head, value_head, grad_head = head_item
        return head_pass(head_index, query_head, key_head, value_head, grad_head, memory_blocks, score_scale)
    merged, grad_query_normed, grad_key_normed, grad_value = lax.map(one_head, (jnp.arange(HEADS, dtype=jnp.int32), split_heads(query_normed), split_heads(key_normed), split_heads(values), split_heads(cotangent)))
    attended = join_heads(merged).astype(jnp.bfloat16)
    query_adjoint = query_gain.astype(jnp.float32) * join_heads(grad_query_normed)
    key_adjoint = key_gain.astype(jnp.float32) * join_heads(grad_key_normed)
    query_inner = lax.optimization_barrier(jnp.sum(query_float * query_adjoint, axis=1, keepdims=True))
    key_inner = lax.optimization_barrier(jnp.sum(key_float * key_adjoint, axis=1, keepdims=True))
    query_grads = (query_inverse * query_adjoint - query_float * query_inverse ** 3 * query_inner / (HEADS * DH)).astype(jnp.bfloat16)
    key_grads = (key_inverse * key_adjoint - key_float * key_inverse ** 3 * key_inner / (HEADS * DH)).astype(jnp.bfloat16)
    value_grads = join_heads(grad_value).astype(jnp.bfloat16)
    return (attended, query_grads, key_grads, value_grads)
```

```python
import functools
import math

import jax
import jax.numpy as jnp
import numpy as np
from jax import lax
from jax.experimental import pallas as pl
from jax.experimental.pallas import tpu as pltpu
from jax.sharding import PartitionSpec as P

DH = 128
D = 4096
LEVELS = 4
BLOCK = 128


EPSILON = 1e-06
FLOOR_SCORE = -1e30


SEG = 512
CLASSES = 8
PER = SEG // CLASSES
ORDER = (0, 4, 2, 6, 1, 3, 5, 7)
SCALE = 1.0 / math.sqrt(DH)
EXP2_SCALE = SCALE * math.log2(math.e)
VMEM_BYTES = 56 * 2**20


def dot_nt(left, right):
    return lax.dot_general(left, right, (((1,), (1,)), ((), ())), preferred_element_type=jnp.float32)


def dot_nn(left, right):
    return lax.dot_general(left, right, (((1,), (0,)), ((), ())), preferred_element_type=jnp.float32)


def dot_tn(left, right):
    return lax.dot_general(left, right, (((0,), (0,)), ((), ())), preferred_element_type=jnp.float32)


def class_matrix():
    matrix = np.zeros((SEG, SEG), np.float32)
    for residue in range(CLASSES):
        for index in range(PER):
            matrix[residue * PER + index, index * CLASSES + residue] = 1.0
    return jnp.asarray(matrix, jnp.bfloat16)


def class_rows(first_head, head, residue):
    start = (first_head + head + residue) % CLASSES * PER
    return pl.ds(start if isinstance(start, int) else pl.multiple_of(start, PER), PER)


def first_class(heads):
    return 0 if heads % CLASSES == 0 else lax.axis_index("head") * heads % CLASSES


def split_kernel(matrix_ref, rows_ref, heads_ref, sorted_ref):
    heads = heads_ref.shape[0]
    first_head = first_class(heads)
    sorted_ref[...] = dot_nn(matrix_ref[...], rows_ref[...]).astype(jnp.bfloat16)
    for head in range(heads):
        for place, residue in enumerate(ORDER):
            heads_ref[head, place * PER : (place + 1) * PER, :] = sorted_ref[
                class_rows(first_head, head, residue), head * DH : (head + 1) * DH
            ]


def join_kernel(matrix_ref, heads_ref, rows_ref, sorted_ref):
    heads = heads_ref.shape[0]
    first_head = first_class(heads)
    for head in range(heads):
        for place, residue in enumerate(ORDER):
            sorted_ref[class_rows(first_head, head, residue), head * DH : (head + 1) * DH] = heads_ref[
                head, place * PER : (place + 1) * PER, :
            ]
    rows_ref[...] = dot_tn(matrix_ref[...], sorted_ref[...]).astype(jnp.bfloat16)


def vmem_call(kernel, outs, scratch=(), operand_count=0, smem_first=False, flops=0):
    specs = [pl.BlockSpec(memory_space=pltpu.VMEM)] * operand_count
    if smem_first:
        specs = [pl.BlockSpec(memory_space=pltpu.SMEM)] + specs[1:]
    return pl.pallas_call(
        kernel,
        out_shape=outs,
        in_specs=specs,
        out_specs=jax.tree.map(lambda _: pl.BlockSpec(memory_space=pltpu.VMEM), outs),
        scratch_shapes=list(scratch),
        cost_estimate=pl.CostEstimate(flops=flops, bytes_accessed=2**23, transcendentals=flops // 512),
        compiler_params=pltpu.CompilerParams(vmem_limit_bytes=VMEM_BYTES),
    )


def split_heads(matrix, rows):
    width = rows.shape[1]
    out = jax.ShapeDtypeStruct((width // DH, SEG, DH), jnp.bfloat16)
    scratch = [pltpu.VMEM((SEG, width), jnp.bfloat16)]
    return vmem_call(split_kernel, out, scratch, operand_count=2, flops=2 * SEG * SEG * width)(matrix, rows)


def join_heads(matrix, heads):
    width = heads.shape[0] * DH
    out = jax.ShapeDtypeStruct((SEG, width), jnp.bfloat16)
    scratch = [pltpu.VMEM((SEG, width), jnp.bfloat16)]
    return vmem_call(join_kernel, out, scratch, operand_count=2, flops=2 * SEG * SEG * width)(matrix, heads)


def take_block(ref, block):
    seg, local = block // (SEG // BLOCK), block % (SEG // BLOCK)
    piece = BLOCK // CLASSES
    rows = ref[seg, :, pl.ds(pl.multiple_of(local * piece, piece), piece), :]
    return rows.reshape(BLOCK, DH)


def add_block(ref, block, term):
    seg, local = block // (SEG // BLOCK), block % (SEG // BLOCK)
    piece = BLOCK // CLASSES
    place = (seg, slice(None), pl.ds(pl.multiple_of(local * piece, piece), piece), slice(None))
    ref[place] = ref[place] + term.reshape(CLASSES, piece, DH)


def take_rows(ref, segs, classes):
    return jnp.concatenate([ref[seg, :classes].reshape(classes * PER, DH) for seg in segs], axis=0)


def take_lanes(ref, segs, count):
    return jnp.concatenate([ref[seg, :, :count] for seg in segs], axis=1)


def part_forward(query_rows, key_rows, value_rows):
    scores = dot_nt(key_rows, query_rows)
    row_max = jnp.max(scores, axis=0, keepdims=True) * EXP2_SCALE
    weights = jnp.exp2(scores * EXP2_SCALE - row_max)
    total = jnp.sum(weights, axis=0, keepdims=True)
    return row_max, total, dot_tn(value_rows, weights.astype(jnp.bfloat16))


def merge_parts(parts):
    joint = functools.reduce(jnp.maximum, [part[0] for part in parts])
    factors = [jnp.exp2(part[0] - joint) for part in parts]
    total = sum(factor * part[1] for factor, part in zip(factors, parts))
    summed = sum(factor * part[2] for factor, part in zip(factors, parts))
    return joint, total, summed


def forward_kernel(
    slots, blocks_ref, query_ref, key_ref, value_ref, query_r_ref, key_r_ref, query_gain_ref, key_gain_ref,
    out_ref, merged_ref, lse_ref, qn_ref, kn_ref, max_ref, total_ref,
):
    segs = query_ref.shape[0]

    def normalise(seg, carry):
        for raw, inverse, gain, normed in (
            (query_ref, query_r_ref, query_gain_ref, qn_ref),
            (key_ref, key_r_ref, key_gain_ref, kn_ref),
        ):
            rows = raw[seg].reshape(SEG, DH).astype(jnp.float32) * inverse[seg] * gain[...]
            normed[seg] = rows.astype(jnp.bfloat16).reshape(CLASSES, PER, DH)
        return carry

    lax.fori_loop(0, segs, normalise, 0)

    def own_and_memory(seg, carry):
        query_rows = take_rows(qn_ref, [seg], CLASSES)
        own = part_forward(query_rows, take_rows(kn_ref, [seg], CLASSES), take_rows(value_ref, [seg], CLASSES))
        listed = [blocks_ref[seg, slot] for slot in range(slots)]
        memory = part_forward(
            query_rows,
            jnp.concatenate([take_block(kn_ref, block) for block in listed], axis=0),
            jnp.concatenate([take_block(value_ref, block) for block in listed], axis=0),
        )
        max_ref[seg], total_ref[seg], merged_ref[seg] = merge_parts([own, memory])
        return carry

    lax.fori_loop(0, segs, own_and_memory, 0)

    def fold(members, count, parts):
        old = (
            take_lanes(max_ref, members, count),
            take_lanes(total_ref, members, count),
            take_lanes(merged_ref, members, count),
        )
        joint, total, summed = merge_parts([old] + parts)
        for place, seg in enumerate(members):
            lanes = slice(place * count, (place + 1) * count)
            max_ref[seg, :, :count] = joint[:, lanes]
            total_ref[seg, :, :count] = total[:, lanes]
            merged_ref[seg, :, :count] = summed[:, lanes]

    def level_one(group, carry):
        members = [2 * group, 2 * group + 1]
        part = part_forward(*(take_rows(ref, members, 4) for ref in (qn_ref, kn_ref, value_ref)))
        fold(members, 4 * PER, [part])
        return carry

    lax.fori_loop(0, segs // 2, level_one, 0)

    def upper_levels(group, carry):
        members = [4 * group + place for place in range(4)]
        key_members = [group // 2 * 8 + place for place in range(8)]
        query_rows, key_rows, value_rows = (take_rows(ref, members, 2) for ref in (qn_ref, kn_ref, value_ref))
        second = part_forward(query_rows, key_rows, value_rows)
        third_max, third_total, third_sum = part_forward(
            query_rows, take_rows(kn_ref, key_members, 1), take_rows(value_ref, key_members, 1)
        )
        inside = lax.broadcasted_iota(jnp.int32, third_max.shape, 1) % (2 * PER) < PER
        third_max = jnp.where(inside, third_max, FLOOR_SCORE)
        fold(members, 2 * PER, [second, (third_max, third_total, third_sum)])
        return carry

    lax.fori_loop(0, segs // 4, upper_levels, 0)

    def finish(seg, carry):
        total = total_ref[seg]
        merged = merged_ref[seg] / total
        merged_ref[seg] = merged
        lse_ref[seg] = max_ref[seg] + jnp.log2(total)
        out_ref[seg] = merged.T.astype(jnp.bfloat16)
        return carry

    lax.fori_loop(0, segs, finish, 0)


def part_backward(query_rows, key_rows, value_rows, grad_rows, lse, delta):
    softmax_rows = jnp.exp2(dot_nt(key_rows, query_rows) * EXP2_SCALE - lse)
    grad_scores = (softmax_rows * (dot_nt(value_rows, grad_rows) - delta)).astype(jnp.bfloat16)
    return (
        dot_tn(key_rows, grad_scores) * SCALE,
        dot_nn(grad_scores, query_rows) * SCALE,
        dot_nn(softmax_rows.astype(jnp.bfloat16), grad_rows),
    )


def backward_kernel(
    slots, blocks_ref, qn_ref, kn_ref, value_ref, grad_ref, merged_ref, lse_ref,
    dq_ref, dk_ref, dv_ref, delta_ref, dqt_ref, dvf_ref,
):
    segs = qn_ref.shape[0]
    own_refs = (qn_ref, kn_ref, value_ref, grad_ref)

    def own_level(seg, carry):
        grad_float = grad_ref[seg].reshape(SEG, DH).astype(jnp.float32)
        delta = jnp.sum(grad_float.T * merged_ref[seg], axis=0, keepdims=True)
        delta_ref[seg] = delta
        dqt, dk, dv = part_backward(*(take_rows(ref, [seg], CLASSES) for ref in own_refs), lse_ref[seg], delta)
        dqt_ref[seg] = dqt
        dk_ref[seg] = dk.reshape(CLASSES, PER, DH)
        dvf_ref[seg] = dv.reshape(CLASSES, PER, DH)
        return carry

    lax.fori_loop(0, segs, own_level, 0)

    def memory(seg, carry):
        query_rows = take_rows(qn_ref, [seg], CLASSES)
        grad_rows = take_rows(grad_ref, [seg], CLASSES)
        for first in range(0, slots, 4):
            listed = [blocks_ref[seg, slot] for slot in range(first, min(first + 4, slots))]
            dqt, dk, dv = part_backward(
                query_rows,
                jnp.concatenate([take_block(kn_ref, block) for block in listed], axis=0),
                jnp.concatenate([take_block(value_ref, block) for block in listed], axis=0),
                grad_rows, lse_ref[seg], delta_ref[seg],
            )
            dqt_ref[seg] = dqt_ref[seg] + dqt
            dk = dk.astype(jnp.bfloat16).astype(jnp.float32)
            dv = dv.astype(jnp.bfloat16).astype(jnp.float32)
            for place, block in enumerate(listed):
                rows = slice(place * BLOCK, (place + 1) * BLOCK)
                add_block(dk_ref, block, dk[rows])
                add_block(dvf_ref, block, dv[rows])
        return carry

    lax.fori_loop(0, segs, memory, 0)

    def spread(members, classes, key_members, key_classes, grads):
        dqt, dk, dv = grads
        count = classes * PER
        for place, seg in enumerate(members):
            dqt_ref[seg, :, :count] = dqt_ref[seg, :, :count] + dqt[:, place * count : (place + 1) * count]
        count = key_classes * PER
        for place, seg in enumerate(key_members):
            rows = slice(place * count, (place + 1) * count)
            shape = (key_classes, PER, DH)
            dk_ref[seg, :key_classes] = dk_ref[seg, :key_classes] + dk[rows].reshape(shape)
            dvf_ref[seg, :key_classes] = dvf_ref[seg, :key_classes] + dv[rows].reshape(shape)

    def level_one(group, carry):
        members = [2 * group, 2 * group + 1]
        grads = part_backward(
            *(take_rows(ref, members, 4) for ref in own_refs),
            take_lanes(lse_ref, members, 4 * PER), take_lanes(delta_ref, members, 4 * PER),
        )
        spread(members, 4, members, 4, grads)
        return carry

    lax.fori_loop(0, segs // 2, level_one, 0)

    def upper_levels(group, carry):
        members = [4 * group + place for place in range(4)]
        key_members = [group // 2 * 8 + place for place in range(8)]
        query_rows, key_rows, value_rows, grad_rows = (take_rows(ref, members, 2) for ref in own_refs)
        lse = take_lanes(lse_ref, members, 2 * PER)
        delta = take_lanes(delta_ref, members, 2 * PER)
        spread(members, 2, members, 2, part_backward(query_rows, key_rows, value_rows, grad_rows, lse, delta))
        inside = lax.broadcasted_iota(jnp.int32, lse.shape, 1) % (2 * PER) < PER
        third = part_backward(
            query_rows, take_rows(kn_ref, key_members, 1), take_rows(value_ref, key_members, 1),
            grad_rows, jnp.where(inside, lse, -FLOOR_SCORE), delta,
        )
        spread(members, 2, key_members, 1, third)
        return carry

    lax.fori_loop(0, segs // 4, upper_levels, 0)

    def finish(seg, carry):
        dq_ref[seg] = dqt_ref[seg].T
        dv_ref[seg] = dvf_ref[seg].reshape(SEG, DH).astype(jnp.bfloat16)
        return carry

    lax.fori_loop(0, segs, finish, 0)


def to_head_order(vector, head):
    parts = vector.reshape(-1, PER, CLASSES)
    rolled = lax.dynamic_slice_in_dim(jnp.concatenate([parts, parts], axis=2), head, CLASSES, axis=2)
    return jnp.stack([rolled[:, :, residue] for residue in ORDER], axis=1).reshape(vector.shape)


def from_head_order(vector, head):
    parts = vector.reshape(-1, CLASSES, PER)
    natural = jnp.stack([parts[:, ORDER.index(residue)] for residue in range(CLASSES)], axis=2)
    doubled = jnp.concatenate([natural, natural], axis=2)
    return lax.dynamic_slice_in_dim(doubled, (CLASSES - head) % CLASSES, CLASSES, axis=2).reshape(vector.shape)


def exchange(heads):
    return lax.all_to_all(heads, "ctx", split_axis=0, concat_axis=0, tiled=True)


def send_heads(heads):
    return exchange(jnp.concatenate([heads] * (lax.axis_size("ctx") // heads.shape[0]), axis=0))


def head_shards(queries, key_states, values, query_gain, key_gain, memory_blocks, cotangent):
    segs, slots = memory_blocks.shape
    heads_local = queries.shape[1] // DH
    local_head = lax.axis_index("ctx") % heads_local
    head = (lax.axis_index("head") * heads_local + local_head) % CLASSES
    matrix = class_matrix()
    query_heads = send_heads(split_heads(matrix, queries))
    key_heads = send_heads(split_heads(matrix, key_states))
    value_heads = send_heads(split_heads(matrix, values))
    grad_heads = send_heads(split_heads(matrix, cotangent))
    squares = jnp.stack(
        [jnp.sum(jnp.square(rows.astype(jnp.float32)), axis=1) for rows in (queries, key_states)]
    )
    squares = lax.psum(squares, "head")
    squares = lax.all_gather(squares, "ctx", axis=1)
    inverse = lax.rsqrt(squares / D + EPSILON)
    inverse = jnp.stack([to_head_order(inverse[0], head), to_head_order(inverse[1], head)])
    gains = [
        lax.dynamic_slice_in_dim(gain, local_head * DH, DH).astype(jnp.float32)[None, :]
        for gain in (query_gain, key_gain)
    ]
    classed = (segs, CLASSES, PER, DH)
    flat = (segs, SEG, DH)
    shape = jax.ShapeDtypeStruct
    pairs = segs * SEG * SEG * 4
    attended, merged, lse, query_normed, key_normed = vmem_call(
        functools.partial(forward_kernel, slots),
        (
            shape(flat, jnp.bfloat16), shape((segs, DH, SEG), jnp.float32), shape((segs, 1, SEG), jnp.float32),
            shape(classed, jnp.bfloat16), shape(classed, jnp.bfloat16),
        ),
        [pltpu.VMEM((segs, 1, SEG), jnp.float32)] * 2,
        operand_count=8, smem_first=True, flops=pairs * DH * 4,
    )(
        memory_blocks, query_heads.reshape(classed), key_heads.reshape(classed), value_heads.reshape(classed),
        inverse[0][:, :, None], inverse[1][:, :, None], *gains,
    )
    attended = exchange(attended)
    dq, dk, dv = vmem_call(
        functools.partial(backward_kernel, slots),
        (shape(flat, jnp.float32), shape(classed, jnp.float32), shape(flat, jnp.bfloat16)),
        [
            pltpu.VMEM((segs, 1, SEG), jnp.float32), pltpu.VMEM((segs, DH, SEG), jnp.float32),
            pltpu.VMEM(classed, jnp.float32),
        ],
        operand_count=7, smem_first=True, flops=pairs * DH * 10,
    )(
        memory_blocks, query_normed, key_normed, value_heads.reshape(classed), grad_heads.reshape(classed),
        merged, lse,
    )
    value_grads = exchange(dv)
    raw = [query_heads.astype(jnp.float32), key_heads.astype(jnp.float32)]
    adjoint = [gains[0] * dq, gains[1] * dk.reshape(flat)]
    inner = jnp.stack([from_head_order(jnp.sum(raw[i] * adjoint[i], axis=2), head) for i in range(2)])
    if segs > heads_local:
        inner = jnp.where(lax.axis_index("ctx") < heads_local, inner, 0.0)
    inner = lax.psum(inner, ("ctx", "head"))
    grads = []
    for i in range(2):
        scale = inverse[i][:, :, None]
        weight = inverse[i] ** 3 * to_head_order(inner[i], head) / D
        grads.append(exchange((scale * adjoint[i] - raw[i] * weight[:, :, None]).astype(jnp.bfloat16)))
    return tuple(join_heads(matrix, heads[:heads_local]) for heads in (attended, grads[0], grads[1], value_grads))


def solution(mesh):
    in_specs = (
        P("ctx", "head"),
        P("ctx", "head"),
        P("ctx", "head"),
        P("head"),
        P("head"),
        P(),
        P("ctx", "head"),
    )
    out_specs = (P("ctx", "head"), P("ctx", "head"), P("ctx", "head"), P("ctx", "head"))
    return jax.shard_map(head_shards, mesh=mesh, in_specs=in_specs, out_specs=out_specs, check_vma=False)
```

```python
import functools
import math

import jax
import jax.numpy as jnp
import numpy as np
from jax import lax
from jax.experimental import pallas as pl
from jax.experimental.pallas import tpu as pltpu
from jax.sharding import PartitionSpec as P

DH = 128
D = 4096
LEVELS = 4
BLOCK = 128


EPSILON = 1e-06
FLOOR_SCORE = -1e30


SEG = 512
CLASSES = 8
PER = SEG // CLASSES
ORDER = (0, 4, 2, 6, 1, 3, 5, 7)
SCALE = 1.0 / math.sqrt(DH)
EXP2_SCALE = SCALE * math.log2(math.e)
VMEM_BYTES = 56 * 2**20


def dot_nt(left, right):
    return lax.dot_general(left, right, (((1,), (1,)), ((), ())), preferred_element_type=jnp.float32)


def dot_nn(left, right):
    return lax.dot_general(left, right, (((1,), (0,)), ((), ())), preferred_element_type=jnp.float32)


def dot_tn(left, right):
    return lax.dot_general(left, right, (((0,), (0,)), ((), ())), preferred_element_type=jnp.float32)


def class_matrix():
    matrix = np.zeros((SEG, SEG), np.float32)
    for residue in range(CLASSES):
        for index in range(PER):
            matrix[residue * PER + index, index * CLASSES + residue] = 1.0
    return jnp.asarray(matrix, jnp.bfloat16)


def class_rows(first_head, head, residue):
    start = (first_head + head + residue) % CLASSES * PER
    return pl.ds(start if isinstance(start, int) else pl.multiple_of(start, PER), PER)


def first_class(heads):
    return 0 if heads % CLASSES == 0 else lax.axis_index("head") * heads % CLASSES


def split_rows(matrix_ref, rows_ref, sorted_ref, heads_ref):
    heads = heads_ref.shape[0]
    first_head = first_class(heads)
    sorted_ref[...] = dot_nn(matrix_ref[...], rows_ref[...]).astype(jnp.bfloat16)
    for head in range(heads):
        for place, residue in enumerate(ORDER):
            heads_ref[head, place * PER : (place + 1) * PER, :] = sorted_ref[
                class_rows(first_head, head, residue), head * DH : (head + 1) * DH
            ]


def join_rows(matrix_ref, heads_ref, sorted_ref, rows_ref):
    heads = rows_ref.shape[1] // DH
    first_head = first_class(heads)
    for head in range(heads):
        for place, residue in enumerate(ORDER):
            sorted_ref[class_rows(first_head, head, residue), head * DH : (head + 1) * DH] = heads_ref[
                head, place * PER : (place + 1) * PER, :
            ]
    rows_ref[...] = dot_tn(matrix_ref[...], sorted_ref[...]).astype(jnp.bfloat16)


def peers_of(axis):
    count, place = lax.axis_size(axis), lax.axis_index(axis)
    return [(step, (place + step) % count) for step in range(1, count)]


def meet_peers():
    barrier = pltpu.get_barrier_semaphore()
    total = 0
    for axis in ("ctx", "head"):
        for _, peer in peers_of(axis):
            pl.semaphore_signal(barrier, inc=1, device_id={axis: peer}, device_id_type=pl.DeviceIdType.MESH)
            total += 1
    pl.semaphore_wait(barrier, total)


def send_all(axis, source_of, target, sems):
    copies = []
    for step, peer in peers_of(axis):
        copy = pltpu.make_async_remote_copy(
            src_ref=source_of(peer),
            dst_ref=target,
            send_sem=sems.at[0, step],
            recv_sem=sems.at[1, step],
            device_id={axis: peer},
            device_id_type=pl.DeviceIdType.MESH,
        )
        copy.start()
        copies.append(copy)
    return copies


def receive_all(copies):
    for copy in copies:
        copy.wait_recv()


def finish_sends(copies):
    for copy in copies:
        copy.wait_send()


def head_residue(heads_local):
    return (lax.axis_index("head") * heads_local + lax.axis_index("ctx") % heads_local) % CLASSES


def row_sums(rows):
    return jnp.sum(rows.T, axis=0, keepdims=True)


def columns(row):
    return jnp.broadcast_to(row, (DH, PER)).T


def inbound_kernel(
    matrix_ref, query_ref, key_ref, value_ref, grad_ref, query_gain_ref, key_gain_ref,
    qn_ref, kn_ref, qh_ref, kh_ref, vh_ref, grad_heads_ref, inverse_ref,
    sorted_ref, send_ref, sums_ref, query_sems, key_sems, value_sems, sums_sems, inverse_sems,
):
    segs, heads_local = vh_ref.shape[0], grad_heads_ref.shape[0]
    me, my_group = lax.axis_index("ctx"), lax.axis_index("head")
    residue = head_residue(heads_local)
    meet_peers()
    sends = []
    for index, (rows_ref, arrived_ref, sems) in enumerate(
        ((query_ref, qh_ref, query_sems), (key_ref, kh_ref, key_sems), (value_ref, vh_ref, value_sems))
    ):
        split_rows(matrix_ref, rows_ref, sorted_ref, send_ref.at[index])
        sends.append(
            send_all("ctx", lambda peer: send_ref.at[index, peer % heads_local], arrived_ref.at[me], sems)
        )
        arrived_ref[me] = send_ref[index, me % heads_local]
        if index < 2:
            squares = jnp.zeros((SEG, DH), jnp.float32)
            for head in range(heads_local):
                block = sorted_ref[:, head * DH : (head + 1) * DH].astype(jnp.float32)
                squares = squares + block * block
            for place in range(CLASSES):
                sums_ref[my_group, index, place : place + 1, :] = row_sums(squares[place * PER : (place + 1) * PER])
        if index == 1:
            sums_sends = send_all("head", lambda peer: sums_ref.at[my_group], sums_ref.at[my_group], sums_sems)
    receive_all(sums_sends)
    total = sums_ref[0]
    for group in range(1, sums_ref.shape[0]):
        total = total + sums_ref[group]
    inverse_ref[me] = lax.rsqrt(total / D + EPSILON)
    inverse_sends = send_all("ctx", lambda peer: inverse_ref.at[me], inverse_ref.at[me], inverse_sems)
    split_rows(matrix_ref, grad_ref, sorted_ref, grad_heads_ref)
    receive_all(inverse_sends)
    for index, (arrived_ref, gain_ref, normed_ref) in enumerate(
        ((qh_ref, query_gain_ref, qn_ref), (kh_ref, key_gain_ref, kn_ref))
    ):
        receive_all(sends[index])

        def normalise(seg, carry):
            for place in range(CLASSES):
                rows = slice(place * PER, (place + 1) * PER)
                inverse = inverse_ref[seg, index, pl.ds((residue + ORDER[place]) % CLASSES, 1), :]
                normed = arrived_ref[seg, rows, :].astype(jnp.float32) * columns(inverse) * gain_ref[...]
                normed_ref[seg, rows, :] = normed.astype(jnp.bfloat16)
            return carry

        lax.fori_loop(0, segs, normalise, 0)
    receive_all(sends[2])
    for copies in sends + [sums_sends, inverse_sends]:
        finish_sends(copies)


def outbound_kernel(
    matrix_ref, attended_ref, dv_ref, dq_ref, dk_ref, qh_ref, kh_ref, inverse_ref, query_gain_ref, key_gain_ref,
    out_ref, query_grads_ref, key_grads_ref, value_grads_ref,
    sorted_ref, send_ref, arrived_ref, inner_ref, inner_in_ref, group_ref, total_ref,
    query_sems, key_sems, value_sems, inner_sems, group_sems, total_sems,
):
    segs, heads_local = dv_ref.shape[0], out_ref.shape[1] // DH
    me, my_group = lax.axis_index("ctx"), lax.axis_index("head")
    residue = head_residue(heads_local)
    pairs = ((qh_ref, dq_ref, query_gain_ref), (kh_ref, dk_ref, key_gain_ref))
    meet_peers()
    sends = [send_all("ctx", lambda peer: dv_ref.at[peer], arrived_ref.at[2, me], value_sems)]
    arrived_ref[2, me] = dv_ref[me]

    def inner_products(seg, carry):
        for index, (raw_ref, grad_ref, gain_ref) in enumerate(pairs):
            for place in range(CLASSES):
                rows = slice(place * PER, (place + 1) * PER)
                product = raw_ref[seg, rows, :].astype(jnp.float32) * (gain_ref[...] * grad_ref[seg, rows, :])
                inner_ref[seg, index, pl.ds((residue + ORDER[place]) % CLASSES, 1), :] = row_sums(product)
        return carry

    lax.fori_loop(0, segs, inner_products, 0)
    inner_sends = send_all("ctx", lambda peer: inner_ref.at[peer], inner_in_ref.at[me], inner_sems)
    inner_in_ref[me] = inner_ref[me]
    receive_all(inner_sends)
    subtotal = inner_in_ref[0]
    for head in range(1, heads_local):
        subtotal = subtotal + inner_in_ref[head]
    group_ref[my_group] = subtotal
    group_sends = send_all("head", lambda peer: group_ref.at[my_group], group_ref.at[my_group], group_sems)
    receive_all(group_sends)
    total = group_ref[0]
    for group in range(1, group_ref.shape[0]):
        total = total + group_ref[group]
    total_ref[me] = total
    total_sends = send_all("ctx", lambda peer: total_ref.at[me], total_ref.at[me], total_sems)
    join_rows(matrix_ref, attended_ref, sorted_ref, out_ref)
    receive_all(total_sends)
    for index, (raw_ref, grad_ref, gain_ref) in enumerate(pairs):

        def final_grads(seg, carry):
            inverse = inverse_ref[seg, index]
            weight = inverse * inverse * inverse * total_ref[seg, index] / D
            inner_ref[seg, index] = weight
            for place in range(CLASSES):
                rows = slice(place * PER, (place + 1) * PER)
                pick = pl.ds((residue + ORDER[place]) % CLASSES, 1)
                adjoint = gain_ref[...] * grad_ref[seg, rows, :]
                raw = raw_ref[seg, rows, :].astype(jnp.float32)
                grads = columns(inverse_ref[seg, index, pick, :]) * adjoint
                grads = grads - raw * columns(inner_ref[seg, index, pick, :])
                send_ref[index, seg, rows, :] = grads.astype(jnp.bfloat16)
            return carry

        if index == 0:
            finish_sends(inner_sends)
        lax.fori_loop(0, segs, final_grads, 0)
        sems = (query_sems, key_sems)[index]
        sends.append(send_all("ctx", lambda peer: send_ref.at[index, peer], arrived_ref.at[index, me], sems))
        arrived_ref[index, me] = send_ref[index, me]
    for copies, slot, rows_ref in zip(sends, (2, 0, 1), (value_grads_ref, query_grads_ref, key_grads_ref)):
        receive_all(copies)
        join_rows(matrix_ref, arrived_ref.at[slot], sorted_ref, rows_ref)
    for copies in sends + [group_sends, total_sends]:
        finish_sends(copies)


def vmem_call(kernel, outs, scratch=(), operand_count=0, smem_first=False, flops=0, collective_id=None):
    specs = [pl.BlockSpec(memory_space=pltpu.VMEM)] * operand_count
    if smem_first:
        specs = [pl.BlockSpec(memory_space=pltpu.SMEM)] + specs[1:]
    return pl.pallas_call(
        kernel,
        out_shape=outs,
        in_specs=specs,
        out_specs=jax.tree.map(lambda _: pl.BlockSpec(memory_space=pltpu.VMEM), outs),
        scratch_shapes=list(scratch),
        cost_estimate=pl.CostEstimate(flops=flops, bytes_accessed=2**23, transcendentals=flops // 512),
        compiler_params=pltpu.CompilerParams(
            vmem_limit_bytes=VMEM_BYTES,
            collective_id=collective_id,
            has_side_effects=collective_id is not None,
        ),
    )


def take_block(ref, block):
    seg, local = block // (SEG // BLOCK), block % (SEG // BLOCK)
    piece = BLOCK // CLASSES
    rows = ref[seg, :, pl.ds(pl.multiple_of(local * piece, piece), piece), :]
    return rows.reshape(BLOCK, DH)


def add_block(ref, block, term):
    seg, local = block // (SEG // BLOCK), block % (SEG // BLOCK)
    piece = BLOCK // CLASSES
    place = (seg, slice(None), pl.ds(pl.multiple_of(local * piece, piece), piece), slice(None))
    ref[place] = ref[place] + term.reshape(CLASSES, piece, DH)


def take_rows(ref, segs, classes):
    return jnp.concatenate([ref[seg, :classes].reshape(classes * PER, DH) for seg in segs], axis=0)


def take_lanes(ref, segs, count):
    return jnp.concatenate([ref[seg, :, :count] for seg in segs], axis=1)


def part_forward(query_rows, key_rows, value_rows):
    scores = dot_nt(key_rows, query_rows)
    row_max = jnp.max(scores, axis=0, keepdims=True) * EXP2_SCALE
    weights = jnp.exp2(scores * EXP2_SCALE - row_max)
    total = jnp.sum(weights, axis=0, keepdims=True)
    return row_max, total, dot_tn(value_rows, weights.astype(jnp.bfloat16))


def merge_parts(parts):
    joint = functools.reduce(jnp.maximum, [part[0] for part in parts])
    factors = [jnp.exp2(part[0] - joint) for part in parts]
    total = sum(factor * part[1] for factor, part in zip(factors, parts))
    summed = sum(factor * part[2] for factor, part in zip(factors, parts))
    return joint, total, summed


def forward_kernel(
    slots, blocks_ref, qn_ref, kn_ref, value_ref, out_ref, merged_ref, lse_ref, max_ref, total_ref,
):
    segs = qn_ref.shape[0]

    def own_and_memory(seg, carry):
        query_rows = take_rows(qn_ref, [seg], CLASSES)
        own = part_forward(query_rows, take_rows(kn_ref, [seg], CLASSES), take_rows(value_ref, [seg], CLASSES))
        listed = [blocks_ref[seg, slot] for slot in range(slots)]
        memory = part_forward(
            query_rows,
            jnp.concatenate([take_block(kn_ref, block) for block in listed], axis=0),
            jnp.concatenate([take_block(value_ref, block) for block in listed], axis=0),
        )
        max_ref[seg], total_ref[seg], merged_ref[seg] = merge_parts([own, memory])
        return carry

    lax.fori_loop(0, segs, own_and_memory, 0)

    def fold(members, count, parts):
        old = (
            take_lanes(max_ref, members, count),
            take_lanes(total_ref, members, count),
            take_lanes(merged_ref, members, count),
        )
        joint, total, summed = merge_parts([old] + parts)
        for place, seg in enumerate(members):
            lanes = slice(place * count, (place + 1) * count)
            max_ref[seg, :, :count] = joint[:, lanes]
            total_ref[seg, :, :count] = total[:, lanes]
            merged_ref[seg, :, :count] = summed[:, lanes]

    def level_one(group, carry):
        members = [2 * group, 2 * group + 1]
        part = part_forward(*(take_rows(ref, members, 4) for ref in (qn_ref, kn_ref, value_ref)))
        fold(members, 4 * PER, [part])
        return carry

    lax.fori_loop(0, segs // 2, level_one, 0)

    def upper_levels(group, carry):
        members = [4 * group + place for place in range(4)]
        key_members = [group // 2 * 8 + place for place in range(8)]
        query_rows, key_rows, value_rows = (take_rows(ref, members, 2) for ref in (qn_ref, kn_ref, value_ref))
        second = part_forward(query_rows, key_rows, value_rows)
        third_max, third_total, third_sum = part_forward(
            query_rows, take_rows(kn_ref, key_members, 1), take_rows(value_ref, key_members, 1)
        )
        inside = lax.broadcasted_iota(jnp.int32, third_max.shape, 1) % (2 * PER) < PER
        third_max = jnp.where(inside, third_max, FLOOR_SCORE)
        fold(members, 2 * PER, [second, (third_max, third_total, third_sum)])
        return carry

    lax.fori_loop(0, segs // 4, upper_levels, 0)

    def finish(seg, carry):
        total = total_ref[seg]
        merged = merged_ref[seg] / total
        merged_ref[seg] = merged
        lse_ref[seg] = max_ref[seg] + jnp.log2(total)
        out_ref[seg] = merged.T.astype(jnp.bfloat16)
        return carry

    lax.fori_loop(0, segs, finish, 0)


def part_backward(query_rows, key_rows, value_rows, grad_rows, lse, delta):
    softmax_rows = jnp.exp2(dot_nt(key_rows, query_rows) * EXP2_SCALE - lse)
    grad_scores = (softmax_rows * (dot_nt(value_rows, grad_rows) - delta)).astype(jnp.bfloat16)
    return (
        dot_tn(key_rows, grad_scores) * SCALE,
        dot_nn(grad_scores, query_rows) * SCALE,
        dot_nn(softmax_rows.astype(jnp.bfloat16), grad_rows),
    )


def backward_kernel(
    slots, blocks_ref, qn_ref, kn_ref, value_ref, grad_ref, merged_ref, lse_ref,
    dq_ref, dk_ref, dv_ref, delta_ref, dqt_ref, dvf_ref,
):
    segs = qn_ref.shape[0]
    own_refs = (qn_ref, kn_ref, value_ref, grad_ref)

    def own_level(seg, carry):
        grad_float = grad_ref[seg].reshape(SEG, DH).astype(jnp.float32)
        delta = jnp.sum(grad_float.T * merged_ref[seg], axis=0, keepdims=True)
        delta_ref[seg] = delta
        dqt, dk, dv = part_backward(*(take_rows(ref, [seg], CLASSES) for ref in own_refs), lse_ref[seg], delta)
        dqt_ref[seg] = dqt
        dk_ref[seg] = dk.reshape(CLASSES, PER, DH)
        dvf_ref[seg] = dv.reshape(CLASSES, PER, DH)
        return carry

    lax.fori_loop(0, segs, own_level, 0)

    def memory(seg, carry):
        query_rows = take_rows(qn_ref, [seg], CLASSES)
        grad_rows = take_rows(grad_ref, [seg], CLASSES)
        for first in range(0, slots, 4):
            listed = [blocks_ref[seg, slot] for slot in range(first, min(first + 4, slots))]
            dqt, dk, dv = part_backward(
                query_rows,
                jnp.concatenate([take_block(kn_ref, block) for block in listed], axis=0),
                jnp.concatenate([take_block(value_ref, block) for block in listed], axis=0),
                grad_rows, lse_ref[seg], delta_ref[seg],
            )
            dqt_ref[seg] = dqt_ref[seg] + dqt
            dk = dk.astype(jnp.bfloat16).astype(jnp.float32)
            dv = dv.astype(jnp.bfloat16).astype(jnp.float32)
            for place, block in enumerate(listed):
                rows = slice(place * BLOCK, (place + 1) * BLOCK)
                add_block(dk_ref, block, dk[rows])
                add_block(dvf_ref, block, dv[rows])
        return carry

    lax.fori_loop(0, segs, memory, 0)

    def spread(members, classes, key_members, key_classes, grads):
        dqt, dk, dv = grads
        count = classes * PER
        for place, seg in enumerate(members):
            dqt_ref[seg, :, :count] = dqt_ref[seg, :, :count] + dqt[:, place * count : (place + 1) * count]
        count = key_classes * PER
        for place, seg in enumerate(key_members):
            rows = slice(place * count, (place + 1) * count)
            shape = (key_classes, PER, DH)
            dk_ref[seg, :key_classes] = dk_ref[seg, :key_classes] + dk[rows].reshape(shape)
            dvf_ref[seg, :key_classes] = dvf_ref[seg, :key_classes] + dv[rows].reshape(shape)

    def level_one(group, carry):
        members = [2 * group, 2 * group + 1]
        grads = part_backward(
            *(take_rows(ref, members, 4) for ref in own_refs),
            take_lanes(lse_ref, members, 4 * PER), take_lanes(delta_ref, members, 4 * PER),
        )
        spread(members, 4, members, 4, grads)
        return carry

    lax.fori_loop(0, segs // 2, level_one, 0)

    def upper_levels(group, carry):
        members = [4 * group + place for place in range(4)]
        key_members = [group // 2 * 8 + place for place in range(8)]
        query_rows, key_rows, value_rows, grad_rows = (take_rows(ref, members, 2) for ref in own_refs)
        lse = take_lanes(lse_ref, members, 2 * PER)
        delta = take_lanes(delta_ref, members, 2 * PER)
        spread(members, 2, members, 2, part_backward(query_rows, key_rows, value_rows, grad_rows, lse, delta))
        inside = lax.broadcasted_iota(jnp.int32, lse.shape, 1) % (2 * PER) < PER
        third = part_backward(
            query_rows, take_rows(kn_ref, key_members, 1), take_rows(value_ref, key_members, 1),
            grad_rows, jnp.where(inside, lse, -FLOOR_SCORE), delta,
        )
        spread(members, 2, key_members, 1, third)
        return carry

    lax.fori_loop(0, segs // 4, upper_levels, 0)

    def finish(seg, carry):
        dq_ref[seg] = dqt_ref[seg].T
        dv_ref[seg] = dvf_ref[seg].reshape(SEG, DH).astype(jnp.bfloat16)
        return carry

    lax.fori_loop(0, segs, finish, 0)


def exchange(heads):
    return lax.all_to_all(heads, "ctx", split_axis=0, concat_axis=0, tiled=True)


def head_shards(queries, key_states, values, query_gain, key_gain, memory_blocks, cotangent):
    segs, slots = memory_blocks.shape
    heads_local = queries.shape[1] // DH
    local_head = lax.axis_index("ctx") % heads_local
    groups = lax.axis_size("head")
    matrix = class_matrix()
    gains = [
        lax.dynamic_slice_in_dim(gain, local_head * DH, DH).astype(jnp.float32)[None, :]
        for gain in (query_gain, key_gain)
    ]
    classed = (segs, CLASSES, PER, DH)
    flat = (segs, SEG, DH)
    width = heads_local * DH
    sums = (2, CLASSES, PER)
    shape = jax.ShapeDtypeStruct
    ctx_sems, head_sems = pltpu.SemaphoreType.DMA((2, segs)), pltpu.SemaphoreType.DMA((2, groups))
    pairs = segs * SEG * SEG * 4
    query_normed, key_normed, query_heads, key_heads, value_heads, grad_heads, inverse = vmem_call(
        inbound_kernel,
        (shape(flat, jnp.bfloat16),) * 5
        + (shape((heads_local, SEG, DH), jnp.bfloat16), shape((segs,) + sums, jnp.float32)),
        [
            pltpu.VMEM((SEG, width), jnp.bfloat16), pltpu.VMEM((3, heads_local, SEG, DH), jnp.bfloat16),
            pltpu.VMEM((groups,) + sums, jnp.float32), ctx_sems, ctx_sems, ctx_sems, head_sems, ctx_sems,
        ],
        operand_count=7, flops=8 * SEG * SEG * width, collective_id=0,
    )(matrix, queries, key_states, values, cotangent, *gains)
    grad_heads = exchange(jnp.concatenate([grad_heads] * (segs // heads_local), axis=0))
    query_normed, key_normed = query_normed.reshape(classed), key_normed.reshape(classed)
    attended, merged, lse = vmem_call(
        functools.partial(forward_kernel, slots),
        (shape(flat, jnp.bfloat16), shape((segs, DH, SEG), jnp.float32), shape((segs, 1, SEG), jnp.float32)),
        [pltpu.VMEM((segs, 1, SEG), jnp.float32)] * 2,
        operand_count=4, smem_first=True, flops=pairs * DH * 4,
    )(memory_blocks, query_normed, key_normed, value_heads.reshape(classed))
    attended = exchange(attended)
    dq, dk, dv = vmem_call(
        functools.partial(backward_kernel, slots),
        (shape(flat, jnp.float32), shape(classed, jnp.float32), shape(flat, jnp.bfloat16)),
        [
            pltpu.VMEM((segs, 1, SEG), jnp.float32), pltpu.VMEM((segs, DH, SEG), jnp.float32),
            pltpu.VMEM(classed, jnp.float32),
        ],
        operand_count=7, smem_first=True, flops=pairs * DH * 10,
    )(
        memory_blocks, query_normed, key_normed, value_heads.reshape(classed), grad_heads.reshape(classed),
        merged, lse,
    )
    return vmem_call(
        outbound_kernel,
        (shape((SEG, width), jnp.bfloat16),) * 4,
        [
            pltpu.VMEM((SEG, width), jnp.bfloat16), pltpu.VMEM((2,) + flat, jnp.bfloat16),
            pltpu.VMEM((3,) + flat, jnp.bfloat16), pltpu.VMEM((segs,) + sums, jnp.float32),
            pltpu.VMEM((segs,) + sums, jnp.float32), pltpu.VMEM((groups,) + sums, jnp.float32),
            pltpu.VMEM((segs,) + sums, jnp.float32),
            ctx_sems, ctx_sems, ctx_sems, ctx_sems, head_sems, ctx_sems,
        ],
        operand_count=10, flops=8 * SEG * SEG * width, collective_id=1,
    )(matrix, attended, dv, dq, dk.reshape(flat), query_heads, key_heads, inverse, *gains)


def solution(mesh):
    in_specs = (
        P("ctx", "head"),
        P("ctx", "head"),
        P("ctx", "head"),
        P("head"),
        P("head"),
        P(),
        P("ctx", "head"),
    )
    out_specs = (P("ctx", "head"), P("ctx", "head"), P("ctx", "head"), P("ctx", "head"))
    return jax.shard_map(head_shards, mesh=mesh, in_specs=in_specs, out_specs=out_specs, check_vma=False)
```

```python
import functools
import math

import jax
import jax.numpy as jnp
import numpy as np
from jax import lax
from jax.experimental import pallas as pl
from jax.experimental.pallas import tpu as pltpu
from jax.sharding import PartitionSpec as P

DH = 128
D = 4096
LEVELS = 4
BLOCK = 128


EPSILON = 1e-06
FLOOR_SCORE = -1e30


SEG = 512
CLASSES = 8
PER = SEG // CLASSES
ORDER = (0, 4, 2, 6, 1, 3, 5, 7)
SCALE = 1.0 / math.sqrt(DH)
EXP2_SCALE = SCALE * math.log2(math.e)
VMEM_BYTES = 56 * 2**20


def dot_nt(left, right):
    return lax.dot_general(left, right, (((1,), (1,)), ((), ())), preferred_element_type=jnp.float32)


def dot_nn(left, right):
    return lax.dot_general(left, right, (((1,), (0,)), ((), ())), preferred_element_type=jnp.float32)


def dot_tn(left, right):
    return lax.dot_general(left, right, (((0,), (0,)), ((), ())), preferred_element_type=jnp.float32)


def class_matrix():
    matrix = np.zeros((SEG, SEG), np.float32)
    for residue in range(CLASSES):
        for index in range(PER):
            matrix[residue * PER + index, index * CLASSES + residue] = 1.0
    return jnp.asarray(matrix, jnp.bfloat16)


def class_rows(first_head, head, residue):
    start = (first_head + head + residue) % CLASSES * PER
    return pl.ds(start if isinstance(start, int) else pl.multiple_of(start, PER), PER)


def first_class(heads):
    return 0 if heads % CLASSES == 0 else lax.axis_index("head") * heads % CLASSES


def split_rows(matrix_ref, rows_ref, sorted_ref, heads_ref):
    heads = heads_ref.shape[0]
    first_head = first_class(heads)
    sorted_ref[...] = dot_nn(matrix_ref[...], rows_ref[...]).astype(jnp.bfloat16)
    for head in range(heads):
        for place, residue in enumerate(ORDER):
            heads_ref[head, place] = sorted_ref[
                class_rows(first_head, head, residue), head * DH : (head + 1) * DH
            ]


def join_rows(matrix_ref, heads_ref, sorted_ref, rows_ref):
    heads = rows_ref.shape[1] // DH
    first_head = first_class(heads)
    for head in range(heads):
        for place, residue in enumerate(ORDER):
            sorted_ref[class_rows(first_head, head, residue), head * DH : (head + 1) * DH] = heads_ref[
                head, place * PER : (place + 1) * PER, :
            ]
    rows_ref[...] = dot_tn(matrix_ref[...], sorted_ref[...]).astype(jnp.bfloat16)


def flip(place, mask, count):
    flipped, bit = 0, 1
    while bit < count:
        flipped = flipped + bit * ((place // bit + mask // bit) % 2)
        bit = 2 * bit
    return flipped


def peers_of(axis):
    count, place = lax.axis_size(axis), lax.axis_index(axis)
    far, near = list(range(count - 1, count // 2 - 1, -1)), list(range(count // 2 - 1, 0, -1))
    masks = [mask for pair in zip(far, near + [0]) for mask in pair if mask]
    return [(mask, flip(place, mask, count)) for mask in masks]


def meet_peers():
    barrier = pltpu.get_barrier_semaphore()
    total = 0
    for axis in ("ctx", "head"):
        for _, peer in peers_of(axis):
            pl.semaphore_signal(barrier, inc=1, device_id={axis: peer}, device_id_type=pl.DeviceIdType.MESH)
            total += 1
    pl.semaphore_wait(barrier, total)


def send_all(axis, source_of, target, sems):
    copies = []
    for step, peer in peers_of(axis):
        copy = pltpu.make_async_remote_copy(
            src_ref=source_of(peer),
            dst_ref=target,
            send_sem=sems.at[0, step],
            recv_sem=sems.at[1, step],
            device_id={axis: peer},
            device_id_type=pl.DeviceIdType.MESH,
        )
        copy.start()
        copies.append(copy)
    return copies


def receive_all(copies):
    for copy in copies:
        copy.wait_recv()


def finish_sends(copies):
    for copy in copies:
        copy.wait_send()


def head_residue(heads_local):
    return (lax.axis_index("head") * heads_local + lax.axis_index("ctx") % heads_local) % CLASSES


def row_sums(rows):
    return jnp.sum(rows.T, axis=0, keepdims=True)


def columns(row):
    return jnp.broadcast_to(row, (DH, PER)).T


def store_block_rows(blocks_ref, seg, place, rows):
    piece = BLOCK // CLASSES
    for local in range(SEG // BLOCK):
        blocks_ref[seg * (SEG // BLOCK) + local, place * piece : (place + 1) * piece, :] = rows[
            local * piece : (local + 1) * piece
        ]


def inbound_kernel(
    slots, blocks_ref, matrix_ref, query_ref, key_ref, value_ref, grad_ref, query_gain_ref, key_gain_ref,
    qn_ref, kn_ref, qh_ref, kh_ref, vh_ref, gh_ref, inverse_ref, out_ref, merged_ref, lse_ref,
    sorted_ref, send_ref, sums_ref, kb_ref, vb_ref, max_ref, total_ref,
    query_sems, key_sems, value_sems, grad_sems, sums_sems, inverse_sems,
):
    segs, heads_local = vh_ref.shape[0], send_ref.shape[1]
    me, my_group = lax.axis_index("ctx"), lax.axis_index("head")
    residue = head_residue(heads_local)
    meet_peers()
    sends = []
    for index, (rows_ref, arrived_ref, sems) in enumerate(
        (
            (query_ref, qh_ref, query_sems), (key_ref, kh_ref, key_sems),
            (value_ref, vh_ref, value_sems), (grad_ref, gh_ref, grad_sems),
        )
    ):
        split_rows(matrix_ref, rows_ref, sorted_ref, send_ref.at[index])
        sends.append(
            send_all("ctx", lambda peer: send_ref.at[index, peer % heads_local], arrived_ref.at[me], sems)
        )
        arrived_ref[me] = send_ref[index, me % heads_local]
        if index < 2:
            squares = jnp.zeros((SEG, DH), jnp.float32)
            for head in range(heads_local):
                block = sorted_ref[:, head * DH : (head + 1) * DH].astype(jnp.float32)
                squares = squares + block * block
            for place in range(CLASSES):
                sums_ref[my_group, index, place : place + 1, :] = row_sums(squares[place * PER : (place + 1) * PER])
        if index == 1:
            sums_sends = send_all("head", lambda peer: sums_ref.at[my_group], sums_ref.at[my_group], sums_sems)
            receive_all(sums_sends)
            total = sums_ref[0]
            for group in range(1, sums_ref.shape[0]):
                total = total + sums_ref[group]
            inverse_ref[me] = lax.rsqrt(total / D + EPSILON)
            inverse_sends = send_all("ctx", lambda peer: inverse_ref.at[me], inverse_ref.at[me], inverse_sems)
    receive_all(inverse_sends)
    for index, (arrived_ref, gain_ref, normed_ref) in enumerate(
        ((qh_ref, query_gain_ref, qn_ref), (kh_ref, key_gain_ref, kn_ref))
    ):
        receive_all(sends[index])

        def normalise(seg, carry):
            for place in range(CLASSES):
                inverse = inverse_ref[seg, index, pl.ds((residue + ORDER[place]) % CLASSES, 1), :]
                normed = arrived_ref[seg, place].astype(jnp.float32) * columns(inverse) * gain_ref[...]
                normed_ref[seg, place] = normed.astype(jnp.bfloat16)
                if index == 1:
                    store_block_rows(kb_ref, seg, place, normed.astype(jnp.bfloat16))
            return carry

        lax.fori_loop(0, segs, normalise, 0)
    receive_all(sends[2])

    def value_blocks(seg, carry):
        for place in range(CLASSES):
            store_block_rows(vb_ref, seg, place, vh_ref[seg, place])
        return carry

    lax.fori_loop(0, segs, value_blocks, 0)
    forward_pass(
        slots, blocks_ref, qn_ref, kn_ref, vh_ref, kb_ref, vb_ref, out_ref, merged_ref, lse_ref, max_ref, total_ref
    )
    receive_all(sends[3])
    for copies in sends + [sums_sends, inverse_sends]:
        finish_sends(copies)


def outbound_kernel(
    matrix_ref, attended_ref, dv_ref, dq_ref, dk_ref, qh_ref, kh_ref, inverse_ref, query_gain_ref, key_gain_ref,
    out_ref, query_grads_ref, key_grads_ref, value_grads_ref,
    sorted_ref, send_ref, arrived_ref, inner_ref, inner_in_ref, group_ref, total_ref,
    query_sems, key_sems, value_sems, inner_sems, group_sems, total_sems,
):
    segs, heads_local = dv_ref.shape[0], out_ref.shape[1] // DH
    me, my_group = lax.axis_index("ctx"), lax.axis_index("head")
    residue = head_residue(heads_local)
    pairs = ((qh_ref, dq_ref, query_gain_ref), (kh_ref, dk_ref, key_gain_ref))
    meet_peers()
    half = SEG // 2
    first_sends = send_all(
        "ctx", lambda peer: dv_ref.at[peer, :half], arrived_ref.at[2, me, :half], value_sems.at[0]
    )
    arrived_ref[2, me] = dv_ref[me]

    def inner_products(seg, carry):
        for index, (raw_ref, grad_ref, gain_ref) in enumerate(pairs):
            for place in range(CLASSES):
                rows = slice(place * PER, (place + 1) * PER)
                product = raw_ref[seg, rows, :].astype(jnp.float32) * (gain_ref[...] * grad_ref[seg, rows, :])
                inner_ref[seg, index, pl.ds((residue + ORDER[place]) % CLASSES, 1), :] = row_sums(product)
        return carry

    lax.fori_loop(0, segs, inner_products, 0)
    inner_sends = send_all("ctx", lambda peer: inner_ref.at[peer], inner_in_ref.at[me], inner_sems)
    second_sends = send_all(
        "ctx", lambda peer: dv_ref.at[peer, half:], arrived_ref.at[2, me, half:], value_sems.at[1]
    )
    sends = [first_sends + second_sends]
    inner_in_ref[me] = inner_ref[me]
    receive_all(inner_sends)
    subtotal = inner_in_ref[0]
    for head in range(1, heads_local):
        subtotal = subtotal + inner_in_ref[head]
    group_ref[my_group] = subtotal
    group_sends = send_all("head", lambda peer: group_ref.at[my_group], group_ref.at[my_group], group_sems)
    receive_all(group_sends)
    total = group_ref[0]
    for group in range(1, group_ref.shape[0]):
        total = total + group_ref[group]
    total_ref[me] = total
    total_sends = send_all("ctx", lambda peer: total_ref.at[me], total_ref.at[me], total_sems)
    join_rows(matrix_ref, attended_ref, sorted_ref, out_ref)
    receive_all(total_sends)
    for index, (raw_ref, grad_ref, gain_ref) in enumerate(pairs):

        def final_grads(seg, carry):
            inverse = inverse_ref[seg, index]
            weight = inverse * inverse * inverse * total_ref[seg, index] / D
            inner_ref[seg, index] = weight
            for place in range(CLASSES):
                rows = slice(place * PER, (place + 1) * PER)
                pick = pl.ds((residue + ORDER[place]) % CLASSES, 1)
                adjoint = gain_ref[...] * grad_ref[seg, rows, :]
                raw = raw_ref[seg, rows, :].astype(jnp.float32)
                grads = columns(inverse_ref[seg, index, pick, :]) * adjoint
                grads = grads - raw * columns(inner_ref[seg, index, pick, :])
                send_ref[index, seg, rows, :] = grads.astype(jnp.bfloat16)
            return carry

        if index == 0:
            finish_sends(inner_sends)
        lax.fori_loop(0, segs, final_grads, 0)
        sems = (query_sems, key_sems)[index]
        sends.append(send_all("ctx", lambda peer: send_ref.at[index, peer], arrived_ref.at[index, me], sems))
        arrived_ref[index, me] = send_ref[index, me]
    for copies, slot, rows_ref in zip(sends, (2, 0, 1), (value_grads_ref, query_grads_ref, key_grads_ref)):
        receive_all(copies)
        join_rows(matrix_ref, arrived_ref.at[slot], sorted_ref, rows_ref)
    for copies in sends + [group_sends, total_sends]:
        finish_sends(copies)


def vmem_call(kernel, outs, scratch=(), operand_count=0, smem_first=False, flops=0, collective_id=None):
    specs = [pl.BlockSpec(memory_space=pltpu.VMEM)] * operand_count
    if smem_first:
        specs = [pl.BlockSpec(memory_space=pltpu.SMEM)] + specs[1:]
    return pl.pallas_call(
        kernel,
        out_shape=outs,
        in_specs=specs,
        out_specs=jax.tree.map(lambda _: pl.BlockSpec(memory_space=pltpu.VMEM), outs),
        scratch_shapes=list(scratch),
        cost_estimate=pl.CostEstimate(flops=flops, bytes_accessed=2**23, transcendentals=flops // 512),
        compiler_params=pltpu.CompilerParams(
            vmem_limit_bytes=VMEM_BYTES,
            collective_id=collective_id,
            has_side_effects=collective_id is not None,
        ),
    )


def take_block(ref, block):
    seg, local = block // (SEG // BLOCK), block % (SEG // BLOCK)
    piece = BLOCK // CLASSES
    rows = ref[seg, :, pl.ds(pl.multiple_of(local * piece, piece), piece), :]
    return rows.reshape(BLOCK, DH)


def add_block(ref, block, term):
    seg, local = block // (SEG // BLOCK), block % (SEG // BLOCK)
    piece = BLOCK // CLASSES
    place = (seg, slice(None), pl.ds(pl.multiple_of(local * piece, piece), piece), slice(None))
    ref[place] = ref[place] + term.reshape(CLASSES, piece, DH)


def take_rows(ref, segs, classes):
    return jnp.concatenate([ref[seg, :classes].reshape(classes * PER, DH) for seg in segs], axis=0)


def take_lanes(ref, segs, count):
    return jnp.concatenate([ref[seg, :, :count] for seg in segs], axis=1)


def part_forward(query_rows, key_rows, value_rows):
    scores = dot_nt(key_rows, query_rows)
    row_max = jnp.max(scores, axis=0, keepdims=True) * EXP2_SCALE
    weights = jnp.exp2(scores * EXP2_SCALE - row_max)
    total = jnp.sum(weights, axis=0, keepdims=True)
    return row_max, total, dot_tn(value_rows, weights.astype(jnp.bfloat16))


def merge_parts(parts):
    joint = functools.reduce(jnp.maximum, [part[0] for part in parts])
    factors = [jnp.exp2(part[0] - joint) for part in parts]
    total = sum(factor * part[1] for factor, part in zip(factors, parts))
    summed = sum(factor * part[2] for factor, part in zip(factors, parts))
    return joint, total, summed


def forward_pass(
    slots, blocks_ref, qn_ref, kn_ref, value_ref, kb_ref, vb_ref, out_ref, merged_ref, lse_ref, max_ref, total_ref,
):
    segs = qn_ref.shape[0]

    def own_and_memory(seg, carry):
        query_rows = take_rows(qn_ref, [seg], CLASSES)
        own = part_forward(query_rows, take_rows(kn_ref, [seg], CLASSES), take_rows(value_ref, [seg], CLASSES))
        listed = [blocks_ref[seg, slot] for slot in range(slots)]
        memory = part_forward(
            query_rows,
            jnp.concatenate([kb_ref[block] for block in listed], axis=0),
            jnp.concatenate([vb_ref[block] for block in listed], axis=0),
        )
        max_ref[seg], total_ref[seg], merged_ref[seg] = merge_parts([own, memory])
        return carry

    lax.fori_loop(0, segs, own_and_memory, 0)

    def fold(members, count, parts):
        old = (
            take_lanes(max_ref, members, count),
            take_lanes(total_ref, members, count),
            take_lanes(merged_ref, members, count),
        )
        joint, total, summed = merge_parts([old] + parts)
        for place, seg in enumerate(members):
            lanes = slice(place * count, (place + 1) * count)
            max_ref[seg, :, :count] = joint[:, lanes]
            total_ref[seg, :, :count] = total[:, lanes]
            merged_ref[seg, :, :count] = summed[:, lanes]

    def level_one(group, carry):
        members = [2 * group, 2 * group + 1]
        part = part_forward(*(take_rows(ref, members, 4) for ref in (qn_ref, kn_ref, value_ref)))
        fold(members, 4 * PER, [part])
        return carry

    lax.fori_loop(0, segs // 2, level_one, 0)

    def upper_levels(group, carry):
        members = [4 * group + place for place in range(4)]
        key_members = [group // 2 * 8 + place for place in range(8)]
        query_rows, key_rows, value_rows = (take_rows(ref, members, 2) for ref in (qn_ref, kn_ref, value_ref))
        second = part_forward(query_rows, key_rows, value_rows)
        third_max, third_total, third_sum = part_forward(
            query_rows, take_rows(kn_ref, key_members, 1), take_rows(value_ref, key_members, 1)
        )
        inside = lax.broadcasted_iota(jnp.int32, third_max.shape, 1) % (2 * PER) < PER
        third_max = jnp.where(inside, third_max, FLOOR_SCORE)
        fold(members, 2 * PER, [second, (third_max, third_total, third_sum)])
        return carry

    lax.fori_loop(0, segs // 4, upper_levels, 0)

    def finish(seg, carry):
        total = total_ref[seg]
        merged = merged_ref[seg] / total
        merged_ref[seg] = merged
        lse_ref[seg] = max_ref[seg] + jnp.log2(total)
        out_ref[seg] = merged.T.astype(jnp.bfloat16)
        return carry

    lax.fori_loop(0, segs, finish, 0)


def part_backward(query_rows, key_rows, value_rows, grad_rows, lse, delta):
    softmax_rows = jnp.exp2(dot_nt(key_rows, query_rows) * EXP2_SCALE - lse)
    grad_scores = (softmax_rows * (dot_nt(value_rows, grad_rows) - delta)).astype(jnp.bfloat16)
    return (
        dot_tn(key_rows, grad_scores) * SCALE,
        dot_nn(grad_scores, query_rows) * SCALE,
        dot_nn(softmax_rows.astype(jnp.bfloat16), grad_rows),
    )


def backward_kernel(
    slots, blocks_ref, qn_ref, kn_ref, value_ref, grad_ref, merged_ref, lse_ref,
    dq_ref, dk_ref, dv_ref, delta_ref, dqt_ref, dvf_ref,
):
    segs = qn_ref.shape[0]
    own_refs = (qn_ref, kn_ref, value_ref, grad_ref)

    def own_level(seg, carry):
        grad_float = grad_ref[seg].reshape(SEG, DH).astype(jnp.float32)
        delta = jnp.sum(grad_float.T * merged_ref[seg], axis=0, keepdims=True)
        delta_ref[seg] = delta
        dqt, dk, dv = part_backward(*(take_rows(ref, [seg], CLASSES) for ref in own_refs), lse_ref[seg], delta)
        dqt_ref[seg] = dqt
        dk_ref[seg] = dk.reshape(CLASSES, PER, DH)
        dvf_ref[seg] = dv.reshape(CLASSES, PER, DH)
        return carry

    lax.fori_loop(0, segs, own_level, 0)

    def memory(seg, carry):
        query_rows = take_rows(qn_ref, [seg], CLASSES)
        grad_rows = take_rows(grad_ref, [seg], CLASSES)
        for first in range(0, slots, 4):
            listed = [blocks_ref[seg, slot] for slot in range(first, min(first + 4, slots))]
            dqt, dk, dv = part_backward(
                query_rows,
                jnp.concatenate([take_block(kn_ref, block) for block in listed], axis=0),
                jnp.concatenate([take_block(value_ref, block) for block in listed], axis=0),
                grad_rows, lse_ref[seg], delta_ref[seg],
            )
            dqt_ref[seg] = dqt_ref[seg] + dqt
            dk = dk.astype(jnp.bfloat16).astype(jnp.float32)
            dv = dv.astype(jnp.bfloat16).astype(jnp.float32)
            for place, block in enumerate(listed):
                rows = slice(place * BLOCK, (place + 1) * BLOCK)
                add_block(dk_ref, block, dk[rows])
                add_block(dvf_ref, block, dv[rows])
        return carry

    lax.fori_loop(0, segs, memory, 0)

    def spread(members, classes, key_members, key_classes, grads):
        dqt, dk, dv = grads
        count = classes * PER
        for place, seg in enumerate(members):
            dqt_ref[seg, :, :count] = dqt_ref[seg, :, :count] + dqt[:, place * count : (place + 1) * count]
        count = key_classes * PER
        for place, seg in enumerate(key_members):
            rows = slice(place * count, (place + 1) * count)
            shape = (key_classes, PER, DH)
            dk_ref[seg, :key_classes] = dk_ref[seg, :key_classes] + dk[rows].reshape(shape)
            dvf_ref[seg, :key_classes] = dvf_ref[seg, :key_classes] + dv[rows].reshape(shape)

    def level_one(group, carry):
        members = [2 * group, 2 * group + 1]
        grads = part_backward(
            *(take_rows(ref, members, 4) for ref in own_refs),
            take_lanes(lse_ref, members, 4 * PER), take_lanes(delta_ref, members, 4 * PER),
        )
        spread(members, 4, members, 4, grads)
        return carry

    lax.fori_loop(0, segs // 2, level_one, 0)

    def upper_levels(group, carry):
        members = [4 * group + place for place in range(4)]
        key_members = [group // 2 * 8 + place for place in range(8)]
        query_rows, key_rows, value_rows, grad_rows = (take_rows(ref, members, 2) for ref in own_refs)
        lse = take_lanes(lse_ref, members, 2 * PER)
        delta = take_lanes(delta_ref, members, 2 * PER)
        spread(members, 2, members, 2, part_backward(query_rows, key_rows, value_rows, grad_rows, lse, delta))
        inside = lax.broadcasted_iota(jnp.int32, lse.shape, 1) % (2 * PER) < PER
        third = part_backward(
            query_rows, take_rows(kn_ref, key_members, 1), take_rows(value_ref, key_members, 1),
            grad_rows, jnp.where(inside, lse, -FLOOR_SCORE), delta,
        )
        spread(members, 2, key_members, 1, third)
        return carry

    lax.fori_loop(0, segs // 4, upper_levels, 0)

    def finish(seg, carry):
        dq_ref[seg] = dqt_ref[seg].T
        dv_ref[seg] = dvf_ref[seg].reshape(SEG, DH).astype(jnp.bfloat16)
        return carry

    lax.fori_loop(0, segs, finish, 0)


def exchange(heads):
    return lax.all_to_all(heads, "ctx", split_axis=0, concat_axis=0, tiled=True)


def head_shards(queries, key_states, values, query_gain, key_gain, memory_blocks, cotangent):
    segs, slots = memory_blocks.shape
    heads_local = queries.shape[1] // DH
    local_head = lax.axis_index("ctx") % heads_local
    groups = lax.axis_size("head")
    matrix = class_matrix()
    gains = [
        lax.dynamic_slice_in_dim(gain, local_head * DH, DH).astype(jnp.float32)[None, :]
        for gain in (query_gain, key_gain)
    ]
    classed = (segs, CLASSES, PER, DH)
    flat = (segs, SEG, DH)
    width = heads_local * DH
    sums = (2, CLASSES, PER)
    shape = jax.ShapeDtypeStruct
    ctx_sems, head_sems = pltpu.SemaphoreType.DMA((2, segs)), pltpu.SemaphoreType.DMA((2, groups))
    pairs = segs * SEG * SEG * 4
    classed_bf16 = shape(classed, jnp.bfloat16)
    query_normed, key_normed, query_heads, key_heads, value_heads, grad_heads, inverse, attended, merged, lse = vmem_call(
        functools.partial(inbound_kernel, slots),
        (classed_bf16,) * 6
        + (
            shape((segs,) + sums, jnp.float32), shape(flat, jnp.bfloat16),
            shape((segs, DH, SEG), jnp.float32), shape((segs, 1, SEG), jnp.float32),
        ),
        [
            pltpu.VMEM((SEG, width), jnp.bfloat16), pltpu.VMEM((4, heads_local, CLASSES, PER, DH), jnp.bfloat16),
            pltpu.VMEM((groups,) + sums, jnp.float32),
            pltpu.VMEM((segs * (SEG // BLOCK), BLOCK, DH), jnp.bfloat16),
            pltpu.VMEM((segs * (SEG // BLOCK), BLOCK, DH), jnp.bfloat16),
            pltpu.VMEM((segs, 1, SEG), jnp.float32), pltpu.VMEM((segs, 1, SEG), jnp.float32),
            ctx_sems, ctx_sems, ctx_sems, ctx_sems, head_sems, ctx_sems,
        ],
        operand_count=8, smem_first=True, flops=pairs * DH * 4, collective_id=0,
    )(memory_blocks, matrix, queries, key_states, values, cotangent, *gains)
    attended = exchange(attended)
    dq, dk, dv = vmem_call(
        functools.partial(backward_kernel, slots),
        (shape(flat, jnp.float32), shape(classed, jnp.float32), shape(flat, jnp.bfloat16)),
        [
            pltpu.VMEM((segs, 1, SEG), jnp.float32), pltpu.VMEM((segs, DH, SEG), jnp.float32),
            pltpu.VMEM(classed, jnp.float32),
        ],
        operand_count=7, smem_first=True, flops=pairs * DH * 10,
    )(
        memory_blocks, query_normed, key_normed, value_heads, grad_heads,
        merged, lse,
    )
    return vmem_call(
        outbound_kernel,
        (shape((SEG, width), jnp.bfloat16),) * 4,
        [
            pltpu.VMEM((SEG, width), jnp.bfloat16), pltpu.VMEM((2,) + flat, jnp.bfloat16),
            pltpu.VMEM((3,) + flat, jnp.bfloat16), pltpu.VMEM((segs,) + sums, jnp.float32),
            pltpu.VMEM((segs,) + sums, jnp.float32), pltpu.VMEM((groups,) + sums, jnp.float32),
            pltpu.VMEM((segs,) + sums, jnp.float32),
            ctx_sems, ctx_sems, pltpu.SemaphoreType.DMA((2, 2, segs)), ctx_sems, head_sems, ctx_sems,
        ],
        operand_count=10, flops=8 * SEG * SEG * width, collective_id=1,
    )(matrix, attended, dv, dq, dk.reshape(flat), query_heads.reshape(flat), key_heads.reshape(flat), inverse, *gains)


def solution(mesh):
    in_specs = (
        P("ctx", "head"),
        P("ctx", "head"),
        P("ctx", "head"),
        P("head"),
        P("head"),
        P(),
        P("ctx", "head"),
    )
    out_specs = (P("ctx", "head"), P("ctx", "head"), P("ctx", "head"), P("ctx", "head"))
    return jax.shard_map(head_shards, mesh=mesh, in_specs=in_specs, out_specs=out_specs, check_vma=False)
```

```python
import functools
import math

import jax
import jax.numpy as jnp
import numpy as np
from jax import lax
from jax.experimental import pallas as pl
from jax.experimental.pallas import tpu as pltpu
from jax.sharding import PartitionSpec as P

DH = 128
D = 4096
LEVELS = 4
BLOCK = 128


EPSILON = 1e-06
FLOOR_SCORE = -1e30


SEG = 512
CLASSES = 8
PER = SEG // CLASSES
ORDER = (0, 4, 2, 6, 1, 3, 5, 7)
SCALE = 1.0 / math.sqrt(DH)
EXP2_SCALE = SCALE * math.log2(math.e)
VMEM_BYTES = 56 * 2**20


def dot_nt(left, right):
    return lax.dot_general(left, right, (((1,), (1,)), ((), ())), preferred_element_type=jnp.float32)


def dot_nn(left, right):
    return lax.dot_general(left, right, (((1,), (0,)), ((), ())), preferred_element_type=jnp.float32)


def dot_tn(left, right):
    return lax.dot_general(left, right, (((0,), (0,)), ((), ())), preferred_element_type=jnp.float32)


def class_matrix():
    matrix = np.zeros((SEG, SEG), np.float32)
    for residue in range(CLASSES):
        for index in range(PER):
            matrix[residue * PER + index, index * CLASSES + residue] = 1.0
    return jnp.asarray(matrix, jnp.bfloat16)


def class_rows(first_head, head, residue):
    start = (first_head + head + residue) % CLASSES * PER
    return pl.ds(start if isinstance(start, int) else pl.multiple_of(start, PER), PER)


def first_class(heads):
    return 0 if heads % CLASSES == 0 else lax.axis_index("head") * heads % CLASSES


def split_rows(matrix_ref, rows_ref, sorted_ref, heads_ref):
    heads = heads_ref.shape[0]
    first_head = first_class(heads)
    sorted_ref[...] = dot_nn(matrix_ref[...], rows_ref[...]).astype(jnp.bfloat16)
    for head in range(heads):
        for place, residue in enumerate(ORDER):
            heads_ref[head, place] = sorted_ref[
                class_rows(first_head, head, residue), head * DH : (head + 1) * DH
            ]


def join_rows(matrix_ref, heads_ref, sorted_ref, rows_ref):
    heads = rows_ref.shape[1] // DH
    first_head = first_class(heads)
    for head in range(heads):
        for place, residue in enumerate(ORDER):
            sorted_ref[class_rows(first_head, head, residue), head * DH : (head + 1) * DH] = heads_ref[
                head, place * PER : (place + 1) * PER, :
            ]
    rows_ref[...] = dot_tn(matrix_ref[...], sorted_ref[...]).astype(jnp.bfloat16)


def flip(place, mask, count):
    flipped, bit = 0, 1
    while bit < count:
        flipped = flipped + bit * ((place // bit + mask // bit) % 2)
        bit = 2 * bit
    return flipped


def peers_of(axis):
    count, place = lax.axis_size(axis), lax.axis_index(axis)
    far, near = list(range(count - 1, count // 2 - 1, -1)), list(range(count // 2 - 1, 0, -1))
    masks = [mask for pair in zip(far, near + [0]) for mask in pair if mask]
    return [(mask, flip(place, mask, count)) for mask in masks]


def meet_peers():
    barrier = pltpu.get_barrier_semaphore()
    total = 0
    for axis in ("ctx", "head"):
        for _, peer in peers_of(axis):
            pl.semaphore_signal(barrier, inc=1, device_id={axis: peer}, device_id_type=pl.DeviceIdType.MESH)
            total += 1
    pl.semaphore_wait(barrier, total)


def send_all(axis, source_of, target, sems):
    copies = []
    for step, peer in peers_of(axis):
        copy = pltpu.make_async_remote_copy(
            src_ref=source_of(peer),
            dst_ref=target,
            send_sem=sems.at[0, step],
            recv_sem=sems.at[1, step],
            device_id={axis: peer},
            device_id_type=pl.DeviceIdType.MESH,
        )
        copy.start()
        copies.append(copy)
    return copies


def receive_all(copies):
    for copy in copies:
        copy.wait_recv()


def finish_sends(copies):
    for copy in copies:
        copy.wait_send()


def head_residue(heads_local):
    return (lax.axis_index("head") * heads_local + lax.axis_index("ctx") % heads_local) % CLASSES


def row_sums(rows):
    return jnp.sum(rows.T, axis=0, keepdims=True)


def columns(row):
    return jnp.broadcast_to(row, (DH, PER)).T


def store_block_rows(blocks_ref, seg, place, rows):
    piece = BLOCK // CLASSES
    for local in range(SEG // BLOCK):
        blocks_ref[seg * (SEG // BLOCK) + local, place * piece : (place + 1) * piece, :] = rows[
            local * piece : (local + 1) * piece
        ]


def inbound_kernel(
    slots, blocks_ref, matrix_ref, query_ref, key_ref, value_ref, grad_ref, query_gain_ref, key_gain_ref,
    qn_ref, kn_ref, qh_ref, kh_ref, vh_ref, gh_ref, inverse_ref, out_ref, merged_ref, lse_ref,
    sorted_ref, send_ref, sums_ref, kb_ref, vb_ref, max_ref, total_ref,
    query_sems, key_sems, value_sems, grad_sems, sums_sems, inverse_sems,
):
    segs, heads_local = vh_ref.shape[0], send_ref.shape[1]
    me, my_group = lax.axis_index("ctx"), lax.axis_index("head")
    residue = head_residue(heads_local)
    meet_peers()
    sends = []
    for index, (rows_ref, arrived_ref, sems) in enumerate(
        (
            (query_ref, qh_ref, query_sems), (key_ref, kh_ref, key_sems),
            (value_ref, vh_ref, value_sems), (grad_ref, gh_ref, grad_sems),
        )
    ):
        split_rows(matrix_ref, rows_ref, sorted_ref, send_ref.at[index])
        sends.append(
            send_all("ctx", lambda peer: send_ref.at[index, peer % heads_local], arrived_ref.at[me], sems)
        )
        arrived_ref[me] = send_ref[index, me % heads_local]
        if index < 2:
            squares = jnp.zeros((SEG, DH), jnp.float32)
            for head in range(heads_local):
                block = sorted_ref[:, head * DH : (head + 1) * DH].astype(jnp.float32)
                squares = squares + block * block
            for place in range(CLASSES):
                sums_ref[my_group, index, place : place + 1, :] = row_sums(squares[place * PER : (place + 1) * PER])
        if index == 1:
            sums_sends = send_all("head", lambda peer: sums_ref.at[my_group], sums_ref.at[my_group], sums_sems)
            receive_all(sums_sends)
            total = sums_ref[0]
            for group in range(1, sums_ref.shape[0]):
                total = total + sums_ref[group]
            inverse_ref[me] = lax.rsqrt(total / D + EPSILON)
            inverse_sends = send_all("ctx", lambda peer: inverse_ref.at[me], inverse_ref.at[me], inverse_sems)
    receive_all(inverse_sends)
    for index, (arrived_ref, gain_ref, normed_ref) in enumerate(
        ((qh_ref, query_gain_ref, qn_ref), (kh_ref, key_gain_ref, kn_ref))
    ):
        receive_all(sends[index])

        def normalise(seg, carry):
            for place in range(CLASSES):
                inverse = inverse_ref[seg, index, pl.ds((residue + ORDER[place]) % CLASSES, 1), :]
                normed = arrived_ref[seg, place].astype(jnp.float32) * columns(inverse) * gain_ref[...]
                normed_ref[seg, place] = normed.astype(jnp.bfloat16)
                if index == 1:
                    store_block_rows(kb_ref, seg, place, normed.astype(jnp.bfloat16))
            return carry

        lax.fori_loop(0, segs, normalise, 0)
    receive_all(sends[2])

    def value_blocks(seg, carry):
        for place in range(CLASSES):
            store_block_rows(vb_ref, seg, place, vh_ref[seg, place])
        return carry

    lax.fori_loop(0, segs, value_blocks, 0)
    forward_pass(
        slots, blocks_ref, qn_ref, kn_ref, vh_ref, kb_ref, vb_ref, out_ref, merged_ref, lse_ref, max_ref, total_ref
    )
    receive_all(sends[3])
    for copies in sends + [sums_sends, inverse_sends]:
        finish_sends(copies)


def outbound_kernel(
    matrix_ref, attended_ref, dqt_in_ref, dk_in_ref, dv_in_ref, qn_ref, kn_ref, value_ref, cotangent_ref, lse_ref,
    delta_ref, qh_ref, kh_ref, inverse_ref, query_gain_ref, key_gain_ref,
    out_ref, query_grads_ref, key_grads_ref, value_grads_ref,
    dq_ref, dk_ref, dv_ref, sorted_ref, send_ref, arrived_ref, inner_ref, inner_in_ref, group_ref, total_ref,
    query_sems, key_sems, value_sems, inner_sems, group_sems, total_sems,
):
    segs, heads_local = dv_ref.shape[0], out_ref.shape[1] // DH
    me, my_group = lax.axis_index("ctx"), lax.axis_index("head")
    residue = head_residue(heads_local)
    pairs = ((qh_ref, dq_ref, query_gain_ref), (kh_ref, dk_ref, key_gain_ref))
    meet_peers()
    half = SEG // 2

    def own_level(seg):
        dqt, dk, dv = part_backward(
            qn_ref[seg], kn_ref[seg], value_ref[seg], cotangent_ref[seg], lse_ref[seg], delta_ref[seg]
        )
        dv_ref[seg] = (dv_in_ref[seg] + dv).astype(jnp.bfloat16)
        dk_ref[seg] = dk_in_ref[seg] + dk
        dq_ref[seg] = (dqt_in_ref[seg] + dqt).T

    def finished_values(seg):
        own_level(seg)
        return dv_ref.at[seg, :half]

    first_sends = send_all("ctx", finished_values, arrived_ref.at[2, me, :half], value_sems.at[0])
    own_level(me)
    arrived_ref[2, me] = dv_ref[me]

    def inner_products(seg, carry):
        for index, (raw_ref, grad_ref, gain_ref) in enumerate(pairs):
            for place in range(CLASSES):
                rows = slice(place * PER, (place + 1) * PER)
                product = raw_ref[seg, rows, :].astype(jnp.float32) * (gain_ref[...] * grad_ref[seg, rows, :])
                inner_ref[seg, index, pl.ds((residue + ORDER[place]) % CLASSES, 1), :] = row_sums(product)
        return carry

    lax.fori_loop(0, segs, inner_products, 0)
    inner_sends = send_all("ctx", lambda peer: inner_ref.at[peer], inner_in_ref.at[me], inner_sems)
    second_sends = send_all(
        "ctx", lambda peer: dv_ref.at[peer, half:], arrived_ref.at[2, me, half:], value_sems.at[1]
    )
    sends = [first_sends + second_sends]
    inner_in_ref[me] = inner_ref[me]
    receive_all(inner_sends)
    subtotal = inner_in_ref[0]
    for head in range(1, heads_local):
        subtotal = subtotal + inner_in_ref[head]
    group_ref[my_group] = subtotal
    group_sends = send_all("head", lambda peer: group_ref.at[my_group], group_ref.at[my_group], group_sems)
    receive_all(group_sends)
    total = group_ref[0]
    for group in range(1, group_ref.shape[0]):
        total = total + group_ref[group]
    total_ref[me] = total
    total_sends = send_all("ctx", lambda peer: total_ref.at[me], total_ref.at[me], total_sems)
    join_rows(matrix_ref, attended_ref, sorted_ref, out_ref)
    receive_all(total_sends)
    for index, (raw_ref, grad_ref, gain_ref) in enumerate(pairs):

        def final_grads(seg, carry):
            inverse = inverse_ref[seg, index]
            weight = inverse * inverse * inverse * total_ref[seg, index] / D
            inner_ref[seg, index] = weight
            for place in range(CLASSES):
                rows = slice(place * PER, (place + 1) * PER)
                pick = pl.ds((residue + ORDER[place]) % CLASSES, 1)
                adjoint = gain_ref[...] * grad_ref[seg, rows, :]
                raw = raw_ref[seg, rows, :].astype(jnp.float32)
                grads = columns(inverse_ref[seg, index, pick, :]) * adjoint
                grads = grads - raw * columns(inner_ref[seg, index, pick, :])
                send_ref[index, seg, rows, :] = grads.astype(jnp.bfloat16)
            return carry

        if index == 0:
            finish_sends(inner_sends)
        lax.fori_loop(0, segs, final_grads, 0)
        sems = (query_sems, key_sems)[index]
        sends.append(send_all("ctx", lambda peer: send_ref.at[index, peer], arrived_ref.at[index, me], sems))
        arrived_ref[index, me] = send_ref[index, me]
    for copies, slot, rows_ref in zip(sends, (2, 0, 1), (value_grads_ref, query_grads_ref, key_grads_ref)):
        receive_all(copies)
        join_rows(matrix_ref, arrived_ref.at[slot], sorted_ref, rows_ref)
    for copies in sends + [group_sends, total_sends]:
        finish_sends(copies)


def vmem_call(kernel, outs, scratch=(), operand_count=0, smem_first=False, flops=0, collective_id=None):
    specs = [pl.BlockSpec(memory_space=pltpu.VMEM)] * operand_count
    if smem_first:
        specs = [pl.BlockSpec(memory_space=pltpu.SMEM)] + specs[1:]
    return pl.pallas_call(
        kernel,
        out_shape=outs,
        in_specs=specs,
        out_specs=jax.tree.map(lambda _: pl.BlockSpec(memory_space=pltpu.VMEM), outs),
        scratch_shapes=list(scratch),
        cost_estimate=pl.CostEstimate(flops=flops, bytes_accessed=2**23, transcendentals=flops // 512),
        compiler_params=pltpu.CompilerParams(
            vmem_limit_bytes=VMEM_BYTES,
            collective_id=collective_id,
            has_side_effects=collective_id is not None,
        ),
    )


def take_block(ref, block):
    seg, local = block // (SEG // BLOCK), block % (SEG // BLOCK)
    piece = BLOCK // CLASSES
    rows = ref[seg, :, pl.ds(pl.multiple_of(local * piece, piece), piece), :]
    return rows.reshape(BLOCK, DH)


def add_block(ref, block, term):
    seg, local = block // (SEG // BLOCK), block % (SEG // BLOCK)
    piece = BLOCK // CLASSES
    place = (seg, slice(None), pl.ds(pl.multiple_of(local * piece, piece), piece), slice(None))
    ref[place] = ref[place] + term.reshape(CLASSES, piece, DH)


def take_rows(ref, segs, classes):
    return jnp.concatenate([ref[seg, :classes].reshape(classes * PER, DH) for seg in segs], axis=0)


def take_lanes(ref, segs, count):
    return jnp.concatenate([ref[seg, :, :count] for seg in segs], axis=1)


def part_forward(query_rows, key_rows, value_rows):
    scores = dot_nt(key_rows, query_rows)
    row_max = jnp.max(scores, axis=0, keepdims=True) * EXP2_SCALE
    weights = jnp.exp2(scores * EXP2_SCALE - row_max)
    total = jnp.sum(weights, axis=0, keepdims=True)
    return row_max, total, dot_tn(value_rows, weights.astype(jnp.bfloat16))


def merge_parts(parts):
    joint = functools.reduce(jnp.maximum, [part[0] for part in parts])
    factors = [jnp.exp2(part[0] - joint) for part in parts]
    total = sum(factor * part[1] for factor, part in zip(factors, parts))
    summed = sum(factor * part[2] for factor, part in zip(factors, parts))
    return joint, total, summed


def forward_pass(
    slots, blocks_ref, qn_ref, kn_ref, value_ref, kb_ref, vb_ref, out_ref, merged_ref, lse_ref, max_ref, total_ref,
):
    segs = qn_ref.shape[0]

    def own_and_memory(seg, carry):
        query_rows = take_rows(qn_ref, [seg], CLASSES)
        own = part_forward(query_rows, take_rows(kn_ref, [seg], CLASSES), take_rows(value_ref, [seg], CLASSES))
        listed = [blocks_ref[seg, slot] for slot in range(slots)]
        memory = part_forward(
            query_rows,
            jnp.concatenate([kb_ref[block] for block in listed], axis=0),
            jnp.concatenate([vb_ref[block] for block in listed], axis=0),
        )
        max_ref[seg], total_ref[seg], merged_ref[seg] = merge_parts([own, memory])
        return carry

    lax.fori_loop(0, segs, own_and_memory, 0)

    def fold(members, count, parts):
        old = (
            take_lanes(max_ref, members, count),
            take_lanes(total_ref, members, count),
            take_lanes(merged_ref, members, count),
        )
        joint, total, summed = merge_parts([old] + parts)
        for place, seg in enumerate(members):
            lanes = slice(place * count, (place + 1) * count)
            max_ref[seg, :, :count] = joint[:, lanes]
            total_ref[seg, :, :count] = total[:, lanes]
            merged_ref[seg, :, :count] = summed[:, lanes]

    def level_one(group, carry):
        members = [2 * group, 2 * group + 1]
        part = part_forward(*(take_rows(ref, members, 4) for ref in (qn_ref, kn_ref, value_ref)))
        fold(members, 4 * PER, [part])
        return carry

    lax.fori_loop(0, segs // 2, level_one, 0)

    def upper_levels(group, carry):
        members = [4 * group + place for place in range(4)]
        key_members = [group // 2 * 8 + place for place in range(8)]
        query_rows, key_rows, value_rows = (take_rows(ref, members, 2) for ref in (qn_ref, kn_ref, value_ref))
        second = part_forward(query_rows, key_rows, value_rows)
        third_max, third_total, third_sum = part_forward(
            query_rows, take_rows(kn_ref, key_members, 1), take_rows(value_ref, key_members, 1)
        )
        inside = lax.broadcasted_iota(jnp.int32, third_max.shape, 1) % (2 * PER) < PER
        third_max = jnp.where(inside, third_max, FLOOR_SCORE)
        fold(members, 2 * PER, [second, (third_max, third_total, third_sum)])
        return carry

    lax.fori_loop(0, segs // 4, upper_levels, 0)

    def finish(seg, carry):
        total = total_ref[seg]
        merged = merged_ref[seg] / total
        merged_ref[seg] = merged
        lse_ref[seg] = max_ref[seg] + jnp.log2(total)
        out_ref[seg] = merged.T.astype(jnp.bfloat16)
        return carry

    lax.fori_loop(0, segs, finish, 0)


def part_backward(query_rows, key_rows, value_rows, grad_rows, lse, delta):
    softmax_rows = jnp.exp2(dot_nt(key_rows, query_rows) * EXP2_SCALE - lse)
    grad_scores = (softmax_rows * (dot_nt(value_rows, grad_rows) - delta)).astype(jnp.bfloat16)
    return (
        dot_tn(key_rows, grad_scores) * SCALE,
        dot_nn(grad_scores, query_rows) * SCALE,
        dot_nn(softmax_rows.astype(jnp.bfloat16), grad_rows),
    )


def backward_kernel(
    slots, blocks_ref, qn_ref, kn_ref, value_ref, grad_ref, merged_ref, lse_ref,
    dqt_ref, dk_ref, dvf_ref, delta_ref,
):
    segs = qn_ref.shape[0]
    own_refs = (qn_ref, kn_ref, value_ref, grad_ref)

    def start(seg, carry):
        grad_float = grad_ref[seg].reshape(SEG, DH).astype(jnp.float32)
        delta = jnp.sum(grad_float.T * merged_ref[seg], axis=0, keepdims=True)
        delta_ref[seg] = delta
        dqt_ref[seg] = jnp.zeros(dqt_ref.shape[1:], jnp.float32)
        dk_ref[seg] = jnp.zeros(dk_ref.shape[1:], jnp.float32)
        dvf_ref[seg] = jnp.zeros(dvf_ref.shape[1:], jnp.float32)
        return carry

    lax.fori_loop(0, segs, start, 0)

    def memory(seg, carry):
        query_rows = take_rows(qn_ref, [seg], CLASSES)
        grad_rows = take_rows(grad_ref, [seg], CLASSES)
        for first in range(0, slots, 4):
            listed = [blocks_ref[seg, slot] for slot in range(first, min(first + 4, slots))]
            dqt, dk, dv = part_backward(
                query_rows,
                jnp.concatenate([take_block(kn_ref, block) for block in listed], axis=0),
                jnp.concatenate([take_block(value_ref, block) for block in listed], axis=0),
                grad_rows, lse_ref[seg], delta_ref[seg],
            )
            dqt_ref[seg] = dqt_ref[seg] + dqt
            dk = dk.astype(jnp.bfloat16).astype(jnp.float32)
            dv = dv.astype(jnp.bfloat16).astype(jnp.float32)
            for place, block in enumerate(listed):
                rows = slice(place * BLOCK, (place + 1) * BLOCK)
                add_block(dk_ref, block, dk[rows])
                add_block(dvf_ref, block, dv[rows])
        return carry

    lax.fori_loop(0, segs, memory, 0)

    def spread(members, classes, key_members, key_classes, grads):
        dqt, dk, dv = grads
        count = classes * PER
        for place, seg in enumerate(members):
            dqt_ref[seg, :, :count] = dqt_ref[seg, :, :count] + dqt[:, place * count : (place + 1) * count]
        count = key_classes * PER
        for place, seg in enumerate(key_members):
            rows = slice(place * count, (place + 1) * count)
            shape = (key_classes, PER, DH)
            dk_ref[seg, :key_classes] = dk_ref[seg, :key_classes] + dk[rows].reshape(shape)
            dvf_ref[seg, :key_classes] = dvf_ref[seg, :key_classes] + dv[rows].reshape(shape)

    def level_one(group, carry):
        members = [2 * group, 2 * group + 1]
        grads = part_backward(
            *(take_rows(ref, members, 4) for ref in own_refs),
            take_lanes(lse_ref, members, 4 * PER), take_lanes(delta_ref, members, 4 * PER),
        )
        spread(members, 4, members, 4, grads)
        return carry

    lax.fori_loop(0, segs // 2, level_one, 0)

    def upper_levels(group, carry):
        members = [4 * group + place for place in range(4)]
        key_members = [group // 2 * 8 + place for place in range(8)]
        query_rows, key_rows, value_rows, grad_rows = (take_rows(ref, members, 2) for ref in own_refs)
        lse = take_lanes(lse_ref, members, 2 * PER)
        delta = take_lanes(delta_ref, members, 2 * PER)
        spread(members, 2, members, 2, part_backward(query_rows, key_rows, value_rows, grad_rows, lse, delta))
        inside = lax.broadcasted_iota(jnp.int32, lse.shape, 1) % (2 * PER) < PER
        third = part_backward(
            query_rows, take_rows(kn_ref, key_members, 1), take_rows(value_ref, key_members, 1),
            grad_rows, jnp.where(inside, lse, -FLOOR_SCORE), delta,
        )
        spread(members, 2, key_members, 1, third)
        return carry

    lax.fori_loop(0, segs // 4, upper_levels, 0)


def exchange(heads):
    return lax.all_to_all(heads, "ctx", split_axis=0, concat_axis=0, tiled=True)


def head_shards(queries, key_states, values, query_gain, key_gain, memory_blocks, cotangent):
    segs, slots = memory_blocks.shape
    heads_local = queries.shape[1] // DH
    local_head = lax.axis_index("ctx") % heads_local
    groups = lax.axis_size("head")
    matrix = class_matrix()
    gains = [
        lax.dynamic_slice_in_dim(gain, local_head * DH, DH).astype(jnp.float32)[None, :]
        for gain in (query_gain, key_gain)
    ]
    classed = (segs, CLASSES, PER, DH)
    flat = (segs, SEG, DH)
    width = heads_local * DH
    sums = (2, CLASSES, PER)
    shape = jax.ShapeDtypeStruct
    ctx_sems, head_sems = pltpu.SemaphoreType.DMA((2, segs)), pltpu.SemaphoreType.DMA((2, groups))
    pairs = segs * SEG * SEG * 4
    classed_bf16 = shape(classed, jnp.bfloat16)
    query_normed, key_normed, query_heads, key_heads, value_heads, grad_heads, inverse, attended, merged, lse = vmem_call(
        functools.partial(inbound_kernel, slots),
        (classed_bf16,) * 6
        + (
            shape((segs,) + sums, jnp.float32), shape(flat, jnp.bfloat16),
            shape((segs, DH, SEG), jnp.float32), shape((segs, 1, SEG), jnp.float32),
        ),
        [
            pltpu.VMEM((SEG, width), jnp.bfloat16), pltpu.VMEM((4, heads_local, CLASSES, PER, DH), jnp.bfloat16),
            pltpu.VMEM((groups,) + sums, jnp.float32),
            pltpu.VMEM((segs * (SEG // BLOCK), BLOCK, DH), jnp.bfloat16),
            pltpu.VMEM((segs * (SEG // BLOCK), BLOCK, DH), jnp.bfloat16),
            pltpu.VMEM((segs, 1, SEG), jnp.float32), pltpu.VMEM((segs, 1, SEG), jnp.float32),
            ctx_sems, ctx_sems, ctx_sems, ctx_sems, head_sems, ctx_sems,
        ],
        operand_count=8, smem_first=True, flops=pairs * DH * 4, collective_id=0,
    )(memory_blocks, matrix, queries, key_states, values, cotangent, *gains)
    attended = exchange(attended)
    dqt, dk, dv, delta = vmem_call(
        functools.partial(backward_kernel, slots),
        (
            shape((segs, DH, SEG), jnp.float32), shape(classed, jnp.float32), shape(classed, jnp.float32),
            shape((segs, 1, SEG), jnp.float32),
        ),
        operand_count=7, smem_first=True, flops=pairs * DH * 10,
    )(memory_blocks, query_normed, key_normed, value_heads, grad_heads, merged, lse)
    own = [array.reshape(flat) for array in (query_normed, key_normed, value_heads, grad_heads)]
    return vmem_call(
        outbound_kernel,
        (shape((SEG, width), jnp.bfloat16),) * 4,
        [
            pltpu.VMEM(flat, jnp.float32), pltpu.VMEM(flat, jnp.float32), pltpu.VMEM(flat, jnp.bfloat16),
            pltpu.VMEM((SEG, width), jnp.bfloat16), pltpu.VMEM((2,) + flat, jnp.bfloat16),
            pltpu.VMEM((3,) + flat, jnp.bfloat16), pltpu.VMEM((segs,) + sums, jnp.float32),
            pltpu.VMEM((segs,) + sums, jnp.float32), pltpu.VMEM((groups,) + sums, jnp.float32),
            pltpu.VMEM((segs,) + sums, jnp.float32),
            ctx_sems, ctx_sems, pltpu.SemaphoreType.DMA((2, 2, segs)), ctx_sems, head_sems, ctx_sems,
        ],
        operand_count=16, flops=8 * SEG * SEG * width, collective_id=1,
    )(
        matrix, attended, dqt, dk.reshape(flat), dv.reshape(flat), *own, lse, delta,
        query_heads.reshape(flat), key_heads.reshape(flat), inverse, *gains,
    )


def solution(mesh):
    in_specs = (
        P("ctx", "head"),
        P("ctx", "head"),
        P("ctx", "head"),
        P("head"),
        P("head"),
        P(),
        P("ctx", "head"),
    )
    out_specs = (P("ctx", "head"), P("ctx", "head"), P("ctx", "head"), P("ctx", "head"))
    return jax.shard_map(head_shards, mesh=mesh, in_specs=in_specs, out_specs=out_specs, check_vma=False)
```
